256 devices in a mesh: wide: 8 (over z_hi, core), narrow: 32 (over y, x, z_lo).
Axes of the slice: x: 4, y: 4, z: 8 (z_hi: 4, z_lo: 2; z = z_hi * 2 + z_lo), core: 2. Of those that a mesh axis runs over, the one named last changes fastest.
Arguments:
- queries: bfloat16 [32768, 2048], P(('narrow', 'wide')), may hold values from -4.5 to 4.5, as said below
- keys: bfloat16 [32768, 2048], P(('narrow', 'wide')), may hold values from -4.5 to 4.5, as said below
- values: bfloat16 [32768, 2048], P(('narrow', 'wide')), may hold values from -6 to 6, as said below
- grad_out: bfloat16 [32768, 2048], P(('narrow', 'wide')), may hold values from -6 to 6, as said below
Outputs:
- attended: bfloat16 [32768, 2048], P(('narrow', 'wide'))
- grad_queries: bfloat16 [32768, 2048], P(('narrow', 'wide'))
- grad_keys: bfloat16 [32768, 2048], P(('narrow', 'wide'))
- grad_values: bfloat16 [32768, 2048], P(('narrow', 'wide'))
The draws below stay inside these ranges and needn't reach their ends.
Inputs may be any that keep to these rules, and one draw needn't show every extreme that they name: Entries of queries stay within this range. Entries of keys stay within this range. Entries of values stay within this range. Entries of grad_out stay within this range.
All inputs are finite; a program needn't handle non-finite values.
Results may differ from the reference program's by a relative error of at most 0.022.
Values may be sent and summed in bfloat16 or wider, within the bound.
No kernel may reach another device: no remote copies, remote signals or barrier semaphores. Data moves between devices by JAX's collectives and lax.ppermute only.
A program may use at most 128 MiB of HBM per device.

```python
import jax
import jax.numpy as jnp
from jax import lax

HEADS = 16
HEAD_DIM = 128
BLOCK = 128
POOL_NEAR = 4
POOL_FAR = 64
FEAT = 2048
NEAR_KEYS = 32
FAR_KEYS = 2
TOKENS = 32768
N_WIDE = 8
N_NARROW = 32


def draw_queries(key, part):
    key = jax.random.fold_in(key, 21)
    result = jnp.clip(jax.random.normal(key, (TOKENS, FEAT), jnp.float32), -4.5, 4.5)
    return result.astype(jnp.bfloat16)


def draw_keys(key, part):
    key = jax.random.fold_in(key, 22)
    group_key, noise_key = jax.random.split(key)
    group_rows = 1.9 * jax.random.normal(group_key, (TOKENS // POOL_FAR, FEAT), jnp.float32)
    noise = 0.5 * jax.random.normal(noise_key, (TOKENS, FEAT), jnp.float32)
    result = jnp.clip(jnp.repeat(group_rows, POOL_FAR, axis=0) + noise, -4.5, 4.5)
    return result.astype(jnp.bfloat16)


def draw_values(key, part):
    key = jax.random.fold_in(key, 23)
    group_key, noise_key = jax.random.split(key)
    group_rows = jax.random.normal(group_key, (TOKENS // POOL_FAR, FEAT), jnp.float32)
    noise = 0.6 * jax.random.normal(noise_key, (TOKENS, FEAT), jnp.float32)
    result = jnp.clip(jnp.repeat(group_rows, POOL_FAR, axis=0) + noise, -6.0, 6.0)
    return result.astype(jnp.bfloat16)


def draw_grad_out(key, part):
    key = jax.random.fold_in(key, 24)
    common_key, noise_key = jax.random.split(key)
    common = 0.8 * jax.random.normal(common_key, (1, FEAT), jnp.float32)
    noise = jax.random.normal(noise_key, (TOKENS, FEAT), jnp.float32)
    result = jnp.clip(common + noise, -6.0, 6.0)
    return result.astype(jnp.bfloat16)


def setup_inputs(seed: int = 0) -> dict:
    streams_of = jax.random.split(jax.random.key(seed), 5)
    queries = draw_queries(jax.random.fold_in(streams_of[4], 71), 0)
    keys = draw_keys(jax.random.fold_in(streams_of[4], 71), 0)
    values = draw_values(jax.random.fold_in(streams_of[4], 71), 0)
    grad_out = draw_grad_out(jax.random.fold_in(streams_of[4], 71), 0)
    return dict(queries=queries, keys=keys, values=values, grad_out=grad_out)


def pool_rows(matrix, factor):
    grouped = matrix.astype(jnp.float32).reshape(-1, factor, matrix.shape[-1])
    return jnp.mean(grouped, axis=1).astype(jnp.bfloat16)


def spread_rows(matrix, factor):
    widened = jnp.broadcast_to(matrix[:, None, :], (matrix.shape[0], factor, matrix.shape[1]))
    return widened.reshape(-1, matrix.shape[1])


def rounded(matrix):
    return lax.optimization_barrier(matrix.astype(jnp.bfloat16)).astype(jnp.float32)


def build_bias(row_count, span_len, far_total, far_span, wide_at, narrow_at):
    row_ids = jnp.arange(row_count, dtype=jnp.int32)
    blocked = jnp.float32(-jnp.inf)
    causal = jnp.where(row_ids[None, :] <= row_ids[:, None], jnp.float32(0.0), blocked)
    near_blocks = jnp.arange(span_len, dtype=jnp.int32) // NEAR_KEYS
    near_bias = jnp.where(near_blocks <= wide_at - 1, jnp.float32(0.0), blocked)
    far_spans = jnp.arange(far_total, dtype=jnp.int32) // far_span
    far_bias = jnp.where(far_spans < narrow_at, jnp.float32(0.0), blocked)
    prior_bias = jnp.where(jnp.zeros((row_count,), jnp.int32) + wide_at > 0, jnp.float32(0.0), blocked)
    rest_bias = jnp.concatenate([near_bias, far_bias, prior_bias])
    spread_bias = jnp.broadcast_to(rest_bias[None, :], (row_count, rest_bias.shape[0]))
    return jnp.concatenate([causal, spread_bias], axis=1)


def attend(query_rows, key_list, value_list, grad_rows, bias):
    score_scale = HEAD_DIM ** -0.5
    query_heads = query_rows.astype(jnp.float32).reshape(BLOCK, HEADS, HEAD_DIM)
    key_heads = key_list.astype(jnp.float32).reshape(-1, HEADS, HEAD_DIM)
    value_heads = value_list.astype(jnp.float32).reshape(-1, HEADS, HEAD_DIM)
    grad_heads = grad_rows.astype(jnp.float32).reshape(BLOCK, HEADS, HEAD_DIM)
    scores = jnp.einsum("qhd,khd->hqk", query_heads, key_heads) * score_scale + bias[None]
    row_max = jnp.max(scores, axis=2, keepdims=True)
    log_total = row_max + jnp.log(jnp.sum(jnp.exp(scores - row_max), axis=2, keepdims=True))
    softmax = jnp.exp(scores - log_total)
    weights = rounded(softmax)
    attended = jnp.einsum("hqk,khd->qhd", weights, value_heads).astype(jnp.bfloat16)
    row_dot = jnp.einsum("qhd,qhd->hq", grad_heads, attended.astype(jnp.float32))
    dprob = jnp.einsum("qhd,khd->hqk", grad_heads, value_heads)
    dscore = rounded(softmax * (dprob - row_dot[:, :, None]))
    grad_query = jnp.einsum("hqk,khd->qhd", dscore, key_heads) * score_scale
    key_terms = jnp.einsum("hqk,qhd->khd", dscore, query_heads) * score_scale
    value_terms = jnp.einsum("hqk,qhd->khd", weights, grad_heads)
    return (attended.reshape(BLOCK, FEAT), grad_query.reshape(BLOCK, FEAT).astype(jnp.bfloat16),
            key_terms.reshape(-1, FEAT), value_terms.reshape(-1, FEAT))


def reference(queries, keys, values, grad_out):
    device_total = N_WIDE * N_NARROW
    near_keys = pool_rows(keys, POOL_NEAR)
    near_values = pool_rows(values, POOL_NEAR)
    far_keys = pool_rows(near_keys, POOL_FAR // POOL_NEAR)
    far_values = pool_rows(near_values, POOL_FAR // POOL_NEAR)
    span_len = N_WIDE * NEAR_KEYS
    far_total = far_keys.shape[0]

    def one_block(carried, device_index):
        acc_near_k, acc_near_v, acc_far_k, acc_far_v = carried
        narrow_at = device_index // N_WIDE
        wide_at = device_index % N_WIDE
        row_start = device_index * BLOCK
        prior_start = jnp.maximum(device_index - 1, 0) * BLOCK
        query_rows = lax.dynamic_slice_in_dim(queries, row_start, BLOCK, 0)
        grad_rows = lax.dynamic_slice_in_dim(grad_out, row_start, BLOCK, 0)
        own_keys = lax.dynamic_slice_in_dim(keys, row_start, BLOCK, 0)
        own_values = lax.dynamic_slice_in_dim(values, row_start, BLOCK, 0)
        prior_keys = lax.dynamic_slice_in_dim(keys, prior_start, BLOCK, 0)
        prior_values = lax.dynamic_slice_in_dim(values, prior_start, BLOCK, 0)
        near_start = narrow_at * span_len
        span_keys = lax.dynamic_slice_in_dim(near_keys, near_start, span_len, 0)
        span_values = lax.dynamic_slice_in_dim(near_values, near_start, span_len, 0)
        key_list = jnp.concatenate([own_keys, span_keys, far_keys, prior_keys], axis=0)
        value_list = jnp.concatenate([own_values, span_values, far_values, prior_values], axis=0)
        bias = build_bias(BLOCK, span_len, far_total, N_WIDE * FAR_KEYS, wide_at, narrow_at)
        attended, grad_query, key_terms, value_terms = attend(query_rows, key_list, value_list, grad_rows, bias)
        near_end = BLOCK + span_len
        far_end = near_end + far_total
        old_k = lax.dynamic_slice_in_dim(acc_near_k, near_start, span_len, 0)
        old_v = lax.dynamic_slice_in_dim(acc_near_v, near_start, span_len, 0)
        acc_near_k = lax.dynamic_update_slice_in_dim(acc_near_k, old_k + rounded(key_terms[BLOCK:near_end]), near_start, 0)
        acc_near_v = lax.dynamic_update_slice_in_dim(acc_near_v, old_v + rounded(value_terms[BLOCK:near_end]), near_start, 0)
        acc_far_k = acc_far_k + rounded(key_terms[near_end:far_end])
        acc_far_v = acc_far_v + rounded(value_terms[near_end:far_end])
        outputs = (attended, grad_query, key_terms[:BLOCK], value_terms[:BLOCK],
                   key_terms[far_end:], value_terms[far_end:])
        return (acc_near_k, acc_near_v, acc_far_k, acc_far_v), outputs

    initial = (jnp.zeros(near_keys.shape, jnp.float32), jnp.zeros(near_keys.shape, jnp.float32),
               jnp.zeros(far_keys.shape, jnp.float32), jnp.zeros(far_keys.shape, jnp.float32))
    device_ids = jnp.arange(device_total, dtype=jnp.int32)
    finals, stacked = lax.scan(one_block, initial, device_ids)
    acc_near_k, acc_near_v, acc_far_k, acc_far_v = finals
    attended, grad_query, own_k, own_v, prior_k, prior_v = stacked
    empty = jnp.zeros((1, BLOCK, FEAT), jnp.float32)
    next_k = jnp.concatenate([prior_k[1:], empty], axis=0).reshape(TOKENS, FEAT)
    next_v = jnp.concatenate([prior_v[1:], empty], axis=0).reshape(TOKENS, FEAT)
    grad_keys = (own_k.reshape(TOKENS, FEAT) + next_k + spread_rows(acc_near_k / POOL_NEAR, POOL_NEAR)
                 + spread_rows(acc_far_k / POOL_FAR, POOL_FAR))
    grad_values = (own_v.reshape(TOKENS, FEAT) + next_v + spread_rows(acc_near_v / POOL_NEAR, POOL_NEAR)
                   + spread_rows(acc_far_v / POOL_FAR, POOL_FAR))
    return (attended.reshape(TOKENS, FEAT), grad_query.reshape(TOKENS, FEAT),
            grad_keys.astype(jnp.bfloat16), grad_values.astype(jnp.bfloat16))
```

```python
import functools

import jax
import jax.numpy as jnp
from jax import lax
from jax.experimental import pallas as pl
from jax.experimental.pallas import tpu as pltpu
from jax.sharding import PartitionSpec as P

HEAD_DIM = 128
BLOCK = 128
NEAR = 4
FAR = 64
NEAR_ROWS = 32
FAR_ROWS = 2
WIDE = 8
NARROW = 32
SPAN = WIDE * BLOCK
SPAN_NEAR = WIDE * NEAR_ROWS
SPAN_FAR = WIDE * FAR_ROWS
FAR_ALL = NARROW * SPAN_FAR
FEAT = 2048
PAIR = 2 * HEAD_DIM
SCALE = HEAD_DIM**-0.5
LOG2E = 1.4426950408889634
BLOCKED = -1e30
F32 = jnp.float32
BF16 = jnp.bfloat16

STEPS = [(2, 0), (2, 1), (1, 0), (3, 0), (1, 1), (3, 1), (0, 1), (0, 0)]
SENT = len(STEPS) - 1


def target(at, step):
    chip, core = step
    return ((at // 2 + chip) % 4) * 2 + (at % 2 + core) % 2


def source(at, step):
    chip, core = step
    return ((at // 2 + 4 - chip) % 4) * 2 + (at % 2 + core) % 2


def send(buffers):
    moved = [
        lax.ppermute(b, "wide", [(s, target(s, step)) for s in range(WIDE)])
        for b, step in zip(buffers[:SENT], STEPS)
    ]
    return moved + [buffers[SENT]]


def nt(a, b):
    return lax.dot_general(a, b, (((1,), (1,)), ((), ())), preferred_element_type=F32)


def nn(a, b):
    return lax.dot_general(a, b, (((1,), (0,)), ((), ())), preferred_element_type=F32)


def tn(a, b):
    return lax.dot_general(a, b, (((0,), (0,)), ((), ())), preferred_element_type=F32)


def pooling(rows, factor):
    shape = (rows, rows * factor)
    group = lax.broadcasted_iota(jnp.int32, shape, 1) // factor
    member = group == lax.broadcasted_iota(jnp.int32, shape, 0)
    return jnp.where(member, F32(1.0 / factor), F32(0.0)).astype(BF16)


def spreading(rows, factor):
    shape = (rows * factor, rows)
    group = lax.broadcasted_iota(jnp.int32, shape, 0) // factor
    member = group == lax.broadcasted_iota(jnp.int32, shape, 1)
    return jnp.where(member, F32(1.0 / factor), F32(0.0)).astype(BF16)


def pack_kernel(at_ref, q_ref, k_ref, v_ref, g_ref, *outs):
    wide_at = at_ref[0]
    far_ref = outs[-1]
    for part, step in enumerate(STEPS):
        to = target(wide_at, step)
        for half in range(2):
            columns = pl.ds(pl.multiple_of(to * PAIR + half * HEAD_DIM, HEAD_DIM), HEAD_DIM)
            out = outs[half * len(STEPS) + part]
            for i, ref in enumerate((k_ref, v_ref, q_ref, g_ref)):
                out[i * BLOCK : (i + 1) * BLOCK, :] = ref[:, columns]
    pool_near = pooling(NEAR_ROWS, NEAR)
    pool_far = pooling(FAR_ROWS, FAR // NEAR)
    for i, ref in enumerate((k_ref, v_ref)):
        near = nn(pool_near, ref[...]).astype(BF16)
        far = nn(pool_far, near).astype(BF16)
        for to in range(WIDE):
            far_ref[to, i * FAR_ROWS : (i + 1) * FAR_ROWS, :] = far[:, to * PAIR : (to + 1) * PAIR]


def pack(at, queries, keys, values, grad_out):
    part = jax.ShapeDtypeStruct((4 * BLOCK, HEAD_DIM), BF16)
    far = jax.ShapeDtypeStruct((WIDE, 2 * FAR_ROWS, PAIR), BF16)
    vmem = pl.BlockSpec(memory_space=pltpu.VMEM)
    outs = pl.pallas_call(
        pack_kernel,
        out_shape=[part] * (2 * len(STEPS)) + [far],
        in_specs=[pl.BlockSpec(memory_space=pltpu.SMEM)] + [vmem] * 4,
        out_specs=[vmem] * (2 * len(STEPS) + 1),
        compiler_params=pltpu.CompilerParams(vmem_limit_bytes=24 << 20),
        name="pack",
    )(at, queries, keys, values, grad_out)
    n = len(STEPS)
    return outs[:n], outs[n : 2 * n], outs[2 * n]


def attend_kernel(half, at_ref, *refs):
    n_steps = len(STEPS)
    ins = refs[:n_steps]
    far_ref = refs[n_steps]
    outs = refs[n_steps + 1 : 2 * n_steps + 1]
    far_out = refs[2 * n_steps + 1]
    (q_s, g_s, k_s, v_s, kn_s, vn_s, kf_s, vf_s, o_s, dq_s, dk_s, dv_s, dkn_s, dvn_s, dkf_s, dvf_s, s_s, w_s, d_s) = refs[2 * n_steps + 2 :]
    wide_at = at_ref[0]
    far_seen = at_ref[1] * SPAN_FAR
    pool_near = pooling(NEAR_ROWS, NEAR)
    for part, step in enumerate(STEPS):
        block = source(wide_at, step)
        rows = pl.ds(pl.multiple_of(block * BLOCK, BLOCK), BLOCK)
        near_rows = pl.ds(pl.multiple_of(block * NEAR_ROWS, NEAR_ROWS), NEAR_ROWS)
        piece = [ins[part][i * BLOCK : (i + 1) * BLOCK, :] for i in range(4)]
        k_s[rows, :], v_s[rows, :], q_s[rows, :], g_s[rows, :] = piece
        kn_s[near_rows, :] = nn(pool_near, piece[0]).astype(BF16)
        vn_s[near_rows, :] = nn(pool_near, piece[1]).astype(BF16)
    lanes = slice(half * HEAD_DIM, (half + 1) * HEAD_DIM)
    kf_s[...] = far_ref[:, :SPAN_FAR, lanes].reshape(FAR_ALL, HEAD_DIM)
    vf_s[...] = far_ref[:, SPAN_FAR:, lanes].reshape(FAR_ALL, HEAD_DIM)
    for ref in (dk_s, dv_s, dkn_s, dvn_s, dkf_s, dvf_s):
        ref[...] = jnp.zeros(ref.shape, F32)

    later = lax.broadcasted_iota(jnp.int32, (BLOCK, BLOCK), 0) > lax.broadcasted_iota(
        jnp.int32, (BLOCK, BLOCK), 1
    )
    far_blocked = lax.broadcasted_iota(jnp.int32, (FAR_ALL, 1), 0) >= far_seen
    far_bias = jnp.where(far_blocked, F32(BLOCKED), F32(0.0))
    exponent = SCALE * LOG2E
    wide2 = 2 * BLOCK

    for pair in range(WIDE // 2):
        q_rows = slice(pair * wide2, (pair + 1) * wide2)
        q, g = q_s[q_rows, :], g_s[q_rows, :]
        near = 2 * NEAR_ROWS * pair + NEAR_ROWS
        far_from = wide2 + near
        total = far_from + FAR_ALL
        lists = []
        for b in range(2):
            block = 2 * pair + b
            lists.append((max(block - 1, 0) * BLOCK, block * BLOCK))
        for b in range(2):
            q_b = q[b * BLOCK : (b + 1) * BLOCK]
            cols = slice(b * BLOCK, (b + 1) * BLOCK)
            before, own = lists[b]
            if before == own:
                s_s[0:BLOCK, cols] = jnp.full((BLOCK, BLOCK), BLOCKED, F32)
            else:
                s_s[0:BLOCK, cols] = nt(k_s[before : before + BLOCK, :], q_b)
            s_s[BLOCK:wide2, cols] = jnp.where(later, F32(BLOCKED), nt(k_s[own : own + BLOCK, :], q_b))
        s_s[wide2:far_from, :] = nt(kn_s[0:near, :], q)
        s_s[far_from - NEAR_ROWS : far_from, 0:BLOCK] = jnp.full((NEAR_ROWS, BLOCK), BLOCKED, F32)
        for i in range(0, FAR_ALL, BLOCK):
            s_s[far_from + i : far_from + i + BLOCK, :] = nt(kf_s[i : i + BLOCK, :], q) + far_bias[i : i + BLOCK]
        chunks = [(0, BLOCK), (BLOCK, BLOCK)]
        chunks += [(wide2 + i, min(BLOCK, near - i)) for i in range(0, near, BLOCK)]
        chunks += [(far_from + i, BLOCK) for i in range(0, FAR_ALL, BLOCK)]
        top = None
        for start, size in chunks:
            here = jnp.max(s_s[start : start + size, :].reshape(size // 8, 8, wide2), axis=0)
            top = here if top is None else jnp.maximum(top, here)
        top = jnp.max(top, axis=0, keepdims=True)
        norm = None
        for start, size in chunks:
            e = jnp.exp2((s_s[start : start + size, :] - top) * exponent)
            s_s[start : start + size, :] = e
            here = jnp.sum(e.reshape(size // 8, 8, wide2), axis=0)
            norm = here if norm is None else norm + here
        inverse = 1.0 / jnp.sum(norm, axis=0, keepdims=True)
        for start, size in chunks:
            e = s_s[start : start + size, :] * inverse
            s_s[start : start + size, :] = e
            w_s[start : start + size, :] = e.astype(BF16)
        sides = []
        for b in range(2):
            cols = slice(b * BLOCK, (b + 1) * BLOCK)
            before, own = lists[b]
            sides.append(
                tn(v_s[before : before + BLOCK, :], w_s[0:BLOCK, cols])
                + tn(v_s[own : own + BLOCK, :], w_s[BLOCK:wide2, cols])
            )
        attended = jnp.concatenate(sides, axis=1)
        attended += tn(vn_s[0:near, :], w_s[wide2:far_from, :])
        attended += tn(vf_s[...], w_s[far_from:total, :])
        attended = attended.astype(BF16).astype(F32)
        o_s[q_rows, :] = attended.T.astype(BF16)
        row_dot = jnp.sum(g.astype(F32).T * attended, axis=0, keepdims=True)

        def put(start, size, cols, dprob, dot):
            d_s[start : start + size, cols] = (s_s[start : start + size, cols] * (dprob - dot)).astype(BF16)

        every = slice(0, wide2)
        for b in range(2):
            g_b = g[b * BLOCK : (b + 1) * BLOCK]
            cols = slice(b * BLOCK, (b + 1) * BLOCK)
            before, own = lists[b]
            put(0, BLOCK, cols, nt(v_s[before : before + BLOCK, :], g_b), row_dot[:, cols])
            put(BLOCK, BLOCK, cols, nt(v_s[own : own + BLOCK, :], g_b), row_dot[:, cols])
        put(wide2, near, every, nt(vn_s[0:near, :], g), row_dot)
        for i in range(0, FAR_ALL, BLOCK):
            put(far_from + i, BLOCK, every, nt(vf_s[i : i + BLOCK, :], g), row_dot)
        sides = []
        for b in range(2):
            cols = slice(b * BLOCK, (b + 1) * BLOCK)
            before, own = lists[b]
            q_b, g_b = q[cols], g[cols]
            sides.append(
                tn(k_s[before : before + BLOCK, :], d_s[0:BLOCK, cols])
                + tn(k_s[own : own + BLOCK, :], d_s[BLOCK:wide2, cols])
            )
            if before != own:
                dk_s[before : before + BLOCK, :] += nn(d_s[0:BLOCK, cols], q_b)
                dv_s[before : before + BLOCK, :] += nn(w_s[0:BLOCK, cols], g_b)
            dk_s[own : own + BLOCK, :] += nn(d_s[BLOCK:wide2, cols], q_b)
            dv_s[own : own + BLOCK, :] += nn(w_s[BLOCK:wide2, cols], g_b)
        grad_query = jnp.concatenate(sides, axis=1)
        grad_query += tn(kn_s[0:near, :], d_s[wide2:far_from, :])
        grad_query += tn(kf_s[...], d_s[far_from:total, :])
        dq_s[q_rows, :] = (grad_query * SCALE).T.astype(BF16)
        dkn_s[0:near, :] += nn(d_s[wide2:far_from, :], q)
        dvn_s[0:near, :] += nn(w_s[wide2:far_from, :], g)
        dkf_s[...] += nn(d_s[far_from:total, :], q)
        dvf_s[...] += nn(w_s[far_from:total, :], g)

    spread_near = spreading(NEAR_ROWS, NEAR)
    for block in range(WIDE):
        rows = slice(block * BLOCK, (block + 1) * BLOCK)
        near_rows = slice(block * NEAR_ROWS, (block + 1) * NEAR_ROWS)
        dk_s[rows, :] = (dk_s[rows, :] + nn(spread_near, dkn_s[near_rows, :].astype(BF16))) * SCALE
        dv_s[rows, :] = dv_s[rows, :] + nn(spread_near, dvn_s[near_rows, :].astype(BF16))
    for part, step in enumerate(STEPS):
        rows = pl.ds(pl.multiple_of(target(wide_at, step) * BLOCK, BLOCK), BLOCK)
        outs[part][0:BLOCK, :] = o_s[rows, :]
        outs[part][BLOCK : 2 * BLOCK, :] = dq_s[rows, :]
        outs[part][2 * BLOCK : 3 * BLOCK, :] = dk_s[rows, :].astype(BF16)
        outs[part][3 * BLOCK :, :] = dv_s[rows, :].astype(BF16)
    far_out[:, :SPAN_FAR, :] = (dkf_s[...] * SCALE).astype(BF16).reshape(NARROW, SPAN_FAR, HEAD_DIM)
    far_out[:, SPAN_FAR:, :] = dvf_s[...].astype(BF16).reshape(NARROW, SPAN_FAR, HEAD_DIM)


def attend(half, at, parts, far):
    n = len(STEPS)
    vmem = pl.BlockSpec(memory_space=pltpu.VMEM)
    bf = lambda rows: pltpu.VMEM((rows, HEAD_DIM), BF16)
    fl = lambda rows: pltpu.VMEM((rows, HEAD_DIM), F32)
    outs = pl.pallas_call(
        functools.partial(attend_kernel, half),
        out_shape=[jax.ShapeDtypeStruct((4 * BLOCK, HEAD_DIM), BF16)] * n
        + [jax.ShapeDtypeStruct((NARROW, 2 * SPAN_FAR, HEAD_DIM), BF16)],
        in_specs=[pl.BlockSpec(memory_space=pltpu.SMEM)] + [vmem] * (n + 1),
        out_specs=[vmem] * (n + 1),
        scratch_shapes=[bf(SPAN)] * 4 + [bf(SPAN_NEAR)] * 2 + [bf(FAR_ALL)] * 2 + [bf(SPAN)] * 2
        + [fl(SPAN)] * 2 + [fl(SPAN_NEAR)] * 2 + [fl(FAR_ALL)] * 2
        + [pltpu.VMEM((SPAN, 2 * BLOCK), F32), pltpu.VMEM((SPAN, 2 * BLOCK), BF16), pltpu.VMEM((SPAN, 2 * BLOCK), BF16)],
        compiler_params=pltpu.CompilerParams(vmem_limit_bytes=32 << 20),
        cost_estimate=pl.CostEstimate(flops=1_600_000_000, bytes_accessed=4 << 20, transcendentals=1 << 20),
        name=f"attend{half}",
    )(at, *parts, far)
    return outs[:n], outs[n]


def unpack_kernel(at_ref, *refs):
    n = len(STEPS)
    ins, far_ref, outs = refs[: 2 * n], refs[2 * n], refs[2 * n + 1 :]
    wide_at = at_ref[0]
    for part, step in enumerate(STEPS):
        block = source(wide_at, step)
        for half in range(2):
            columns = pl.ds(pl.multiple_of(block * PAIR + half * HEAD_DIM, HEAD_DIM), HEAD_DIM)
            piece = ins[half * n + part]
            outs[0][:, columns] = piece[0:BLOCK, :]
            outs[1][:, columns] = piece[BLOCK : 2 * BLOCK, :]
            far = far_ref[block, :, half * HEAD_DIM : (half + 1) * HEAD_DIM].astype(F32) * (1.0 / FAR)
            for i in range(2):
                terms = piece[(2 + i) * BLOCK : (3 + i) * BLOCK, :].astype(F32)
                rows = [
                    terms[r * FAR : (r + 1) * FAR] + far[i * FAR_ROWS + r : i * FAR_ROWS + r + 1]
                    for r in range(FAR_ROWS)
                ]
                outs[2 + i][:, columns] = jnp.concatenate(rows, axis=0).astype(BF16)


def unpack(at, parts, far):
    n = len(STEPS)
    vmem = pl.BlockSpec(memory_space=pltpu.VMEM)
    return pl.pallas_call(
        unpack_kernel,
        out_shape=[jax.ShapeDtypeStruct((BLOCK, FEAT), BF16)] * 4,
        in_specs=[pl.BlockSpec(memory_space=pltpu.SMEM)] + [vmem] * (2 * n + 1),
        out_specs=[vmem] * 4,
        compiler_params=pltpu.CompilerParams(vmem_limit_bytes=24 << 20),
        name="unpack",
    )(at, *parts, far)


def shards(queries, keys, values, grad_out):
    at = jnp.stack([lax.axis_index("wide"), lax.axis_index("narrow")]).astype(jnp.int32)
    first, second, far = pack(at, queries, keys, values, grad_out)
    first = send(first)
    far = lax.all_to_all(far, "wide", 0, 0, tiled=True)
    far = far.reshape(WIDE, 2, FAR_ROWS, PAIR).transpose(1, 0, 2, 3).reshape(1, 2 * SPAN_FAR, PAIR)
    far = jnp.broadcast_to(far, (NARROW, 2 * SPAN_FAR, PAIR))
    far = lax.all_to_all(far, "narrow", 0, 0, tiled=True)
    chained = lax.optimization_barrier(tuple(first) + tuple(second))
    first, second = list(chained[: len(STEPS)]), list(chained[len(STEPS) :])
    second = send(second)
    first, far_first = attend(0, at, first, far)
    first = send(first)
    second, far_second = attend(1, at, second, far)
    second = send(second)
    far = jnp.concatenate([far_first, far_second], axis=2)
    far = lax.all_to_all(far, "narrow", 0, 0, tiled=True)
    far = jnp.sum(far.astype(F32), axis=0).astype(BF16)
    far = far.reshape(2, WIDE, FAR_ROWS, PAIR).transpose(1, 0, 2, 3).reshape(WIDE, 2 * FAR_ROWS, PAIR)
    far = lax.all_to_all(far, "wide", 0, 0, tiled=True)
    return tuple(unpack(at, list(first) + list(second), far))


def solution(mesh):
    rows = P(("narrow", "wide"), None)
    return jax.shard_map(
        shards, mesh=mesh, in_specs=(rows,) * 4, out_specs=(rows,) * 4, check_vma=False
    )
```

```python
import functools

import jax
import jax.numpy as jnp
from jax import lax
from jax.experimental import pallas as pl
from jax.experimental.pallas import tpu as pltpu
from jax.sharding import PartitionSpec as P

HEAD_DIM = 128
BLOCK = 128
NEAR = 4
FAR = 64
NEAR_ROWS = 32
FAR_ROWS = 2
WIDE = 8
NARROW = 32
SPAN = WIDE * BLOCK
SPAN_NEAR = WIDE * NEAR_ROWS
SPAN_FAR = WIDE * FAR_ROWS
FAR_ALL = NARROW * SPAN_FAR
FEAT = 2048
PAIR = 2 * HEAD_DIM
SCALE = HEAD_DIM**-0.5
LOG2E = 1.4426950408889634
BLOCKED = -1e30
F32 = jnp.float32
BF16 = jnp.bfloat16

CHIPS = [1, 3, 2, 0]
SENT = len(CHIPS) - 1
HALF = 4 * BLOCK
TAIL = 16
STEPS = [(chip, core) for core in range(2) for chip in CHIPS]


def target(at, step):
    chip, core = step
    return ((at // 2 + chip) % 4) * 2 + (at % 2 + core) % 2


def source(at, step):
    chip, core = step
    return ((at // 2 + 4 - chip) % 4) * 2 + (at % 2 + core) % 2


def move(buffer, step):
    return lax.ppermute(buffer, "wide", [(s, target(s, step)) for s in range(WIDE)])


def to_chips(parts):
    return [move(part, (chip, 0)) for part, chip in zip(parts[:SENT], CHIPS)] + [parts[SENT]]


def to_other_core(parts):
    return move(gather_halves(parts), (0, 1))


def after(values, others):
    tied = lax.optimization_barrier((list(values), list(others)))
    return tied[0], tied[1]


def copy_all(pairs, sems):
    copies = [pltpu.make_async_copy(src, dst, sems.at[i]) for i, (src, dst) in enumerate(pairs)]
    for copy in copies:
        copy.start()
    return copies


def gather_kernel(*refs):
    n = len(refs) - 2
    ins, out, sems = refs[:n], refs[n], refs[n + 1]
    pairs, row = [], 0
    for ref in ins:
        half = ref.shape[0] // 2
        pairs.append((ref.at[pl.ds(half, half), :], out.at[pl.ds(row, half), :]))
        row += half
    for copy in copy_all(pairs, sems):
        copy.wait()


def gather_halves(parts):
    n = len(parts)
    some = pl.BlockSpec(memory_space=pl.ANY)
    return pl.pallas_call(
        gather_kernel,
        out_shape=jax.ShapeDtypeStruct((sum(part.shape[0] for part in parts) // 2, HEAD_DIM), BF16),
        in_specs=[some] * n,
        out_specs=some,
        scratch_shapes=[pltpu.SemaphoreType.DMA((n,))],
        compiler_params=pltpu.CompilerParams(vmem_limit_bytes=1 << 20),
        name="gather_halves",
    )(*parts)


def nt(a, b):
    return lax.dot_general(a, b, (((1,), (1,)), ((), ())), preferred_element_type=F32)


def nn(a, b):
    return lax.dot_general(a, b, (((1,), (0,)), ((), ())), preferred_element_type=F32)


def tn(a, b):
    return lax.dot_general(a, b, (((0,), (0,)), ((), ())), preferred_element_type=F32)


def pooling(rows, factor):
    shape = (rows, rows * factor)
    group = lax.broadcasted_iota(jnp.int32, shape, 1) // factor
    member = group == lax.broadcasted_iota(jnp.int32, shape, 0)
    return jnp.where(member, F32(1.0 / factor), F32(0.0)).astype(BF16)


def spreading(rows, factor):
    shape = (rows * factor, rows)
    group = lax.broadcasted_iota(jnp.int32, shape, 0) // factor
    member = group == lax.broadcasted_iota(jnp.int32, shape, 1)
    return jnp.where(member, F32(1.0 / factor), F32(0.0)).astype(BF16)


def pack_kernel(at_ref, k_ref, v_ref, q_ref, g_ref, *refs):
    n = len(CHIPS)
    outs, (held, staged, far_s, in_sems, out_sems) = refs[: 2 * n], refs[2 * n :]
    wide_at = at_ref[0]
    strip = BLOCK // 4
    pairs = []
    for i, ref in enumerate((k_ref, v_ref, q_ref, g_ref)):
        for r in range(0, BLOCK, strip):
            pairs.append((ref.at[r : r + strip, :], held.at[i, r : r + strip, :]))
    copies = copy_all(pairs, in_sems)
    for copy in copies[:8]:
        copy.wait()
    pool_near = pooling(NEAR_ROWS, NEAR)
    group = lax.broadcasted_iota(jnp.int32, (TAIL, NEAR_ROWS), 1) // (FAR // NEAR)
    row = lax.broadcasted_iota(jnp.int32, (TAIL, NEAR_ROWS), 0)
    far = None
    for i in range(2):
        near = nn(pool_near, held[i]).astype(BF16)
        pool_far = jnp.where(row == group + i * FAR_ROWS, F32(NEAR / FAR), F32(0.0)).astype(BF16)
        far = nn(pool_far, near) if far is None else far + nn(pool_far, near)
    far_s[...] = far.astype(BF16)
    for copy in copies[8:]:
        copy.wait()
    last = []
    for head in range(2):
        half = HALF + 2 * TAIL * (1 - head)
        for part, chip in enumerate(CHIPS):
            at = head * n + part
            for core in range(2):
                column = target(wide_at, (chip, core)) * PAIR
                columns = pl.ds(pl.multiple_of(column + head * HEAD_DIM, HEAD_DIM), HEAD_DIM)
                for i in range(4):
                    row = core * half + i * BLOCK
                    staged[at, row : row + BLOCK, :] = held[i, :, columns]
                if head == 0:
                    for j in range(2):
                        row = core * half + HALF + j * TAIL
                        columns = pl.ds(pl.multiple_of(column + j * HEAD_DIM, HEAD_DIM), HEAD_DIM)
                        staged[at, row : row + TAIL, :] = far_s[:, columns]
            copy = pltpu.make_async_copy(staged.at[at, pl.ds(0, 2 * half), :], outs[at], out_sems.at[at])
            copy.start()
            last.append(copy)
    for copy in last:
        copy.wait()


def pack(at, queries, keys, values, grad_out):
    n = len(CHIPS)
    shapes = [jax.ShapeDtypeStruct((2 * HALF + extra, HEAD_DIM), BF16) for extra in (4 * TAIL, 0)]
    some = pl.BlockSpec(memory_space=pl.ANY)
    outs = pl.pallas_call(
        pack_kernel,
        out_shape=[shapes[0]] * n + [shapes[1]] * n,
        in_specs=[pl.BlockSpec(memory_space=pltpu.SMEM)] + [some] * 4,
        out_specs=[some] * (2 * n),
        scratch_shapes=[
            pltpu.VMEM((4, BLOCK, FEAT), BF16),
            pltpu.VMEM((2 * n, *shapes[0].shape), BF16),
            pltpu.VMEM((TAIL, FEAT), BF16),
            pltpu.SemaphoreType.DMA((16,)),
            pltpu.SemaphoreType.DMA((2 * n,)),
        ],
        compiler_params=pltpu.CompilerParams(vmem_limit_bytes=58 << 20),
        cost_estimate=pl.CostEstimate(flops=0, bytes_accessed=4 << 20, transcendentals=0),
        name="pack",
    )(at, keys, values, queries, grad_out)
    return outs[:n], outs[n:]


def arrivals(parts, swapped, place, start=0, rows=HALF):
    n = len(CHIPS)
    half = parts[0].shape[0] // 2
    pairs = [(parts[i].at[pl.ds(start, rows), :], place(i)) for i in range(n)]
    return pairs + [(swapped.at[pl.ds(i * half + start, rows), :], place(n + i)) for i in range(n)]


def collect_kernel(at_ref, *refs):
    n = len(CHIPS)
    ins, swapped, out, held, sems = refs[:n], refs[n], refs[n + 1], refs[n + 2], refs[n + 3]
    wide_at = at_ref[0]
    pairs = []
    for head in range(2):
        place = lambda i: held.at[head, source(wide_at, STEPS[i])]
        pairs += arrivals(ins, swapped, place, HALF + head * TAIL, TAIL)
    for copy in copy_all(pairs, sems):
        copy.wait()
    shape = (2 * SPAN_FAR, WIDE * TAIL)
    row, column = lax.broadcasted_iota(jnp.int32, shape, 0), lax.broadcasted_iota(jnp.int32, shape, 1)
    inner = row % SPAN_FAR
    wanted = (inner // FAR_ROWS) * TAIL + inner % FAR_ROWS + (row // SPAN_FAR) * FAR_ROWS
    choose = jnp.where(column == wanted, F32(1.0), F32(0.0)).astype(BF16)
    for head in range(2):
        rows = nn(choose, held[head].reshape(WIDE * TAIL, HEAD_DIM)).astype(BF16)
        mine = slice(2 * head * SPAN_FAR, 2 * (head + 1) * SPAN_FAR)
        out[:, mine, :] = jnp.broadcast_to(rows[None], (NARROW, 2 * SPAN_FAR, HEAD_DIM))


def collect(at, parts, swapped):
    n = len(CHIPS)
    return pl.pallas_call(
        collect_kernel,
        out_shape=jax.ShapeDtypeStruct((NARROW, 4 * SPAN_FAR, HEAD_DIM), BF16),
        in_specs=[pl.BlockSpec(memory_space=pltpu.SMEM)] + [pl.BlockSpec(memory_space=pl.ANY)] * (n + 1),
        out_specs=pl.BlockSpec(memory_space=pltpu.VMEM),
        scratch_shapes=[pltpu.VMEM((2, WIDE, TAIL, HEAD_DIM), BF16), pltpu.SemaphoreType.DMA((2 * WIDE,))],
        compiler_params=pltpu.CompilerParams(vmem_limit_bytes=4 << 20),
        name="collect",
    )(at, *parts, swapped)


def attend_kernel(head, at_ref, *refs):
    n = len(CHIPS)
    ins, swapped, far_ref, refs = refs[:n], refs[n], refs[n + 1], refs[n + 2 :]
    if head:
        other_far, refs = refs[0], refs[1:]
    outs, far_out = refs[:n], refs[n]
    held, kn_s, vn_s, o_s, dq_s, dk_s, dv_s, dkn_s, dvn_s, dkf_s, dvf_s, s_s, w_s, d_s, sems = refs[n + 1 :]
    wide_at = at_ref[0]
    far_seen = at_ref[1] * SPAN_FAR
    copies = copy_all(arrivals(ins, swapped, lambda i: held.at[source(wide_at, STEPS[i])]), sems)
    for ref in (dk_s, dv_s, dkn_s, dvn_s, dkf_s, dvf_s):
        ref[...] = jnp.zeros(ref.shape, F32)
    for copy in copies:
        copy.wait()
    pool_near = pooling(NEAR_ROWS, NEAR)
    spread_near = spreading(NEAR_ROWS, NEAR)
    later = lax.broadcasted_iota(jnp.int32, (BLOCK, BLOCK), 0) > lax.broadcasted_iota(
        jnp.int32, (BLOCK, BLOCK), 1
    )
    far_blocked = lax.broadcasted_iota(jnp.int32, (FAR_ALL, 1), 0) >= far_seen
    far_bias = jnp.where(far_blocked, F32(BLOCKED), F32(0.0))
    exponent = SCALE * LOG2E
    wide2 = 2 * BLOCK
    first = 2 * head * SPAN_FAR
    kf = far_ref[:, first : first + SPAN_FAR, :].reshape(FAR_ALL, HEAD_DIM)
    vf = far_ref[:, first + SPAN_FAR : first + 2 * SPAN_FAR, :].reshape(FAR_ALL, HEAD_DIM)

    def rows_of(array, block):
        row = array * BLOCK
        return held[block, row : row + BLOCK, :]

    key = functools.partial(rows_of, 0)
    value = functools.partial(rows_of, 1)
    query = functools.partial(rows_of, 2)
    grad = functools.partial(rows_of, 3)
    for block in range(WIDE):
        near_rows = slice(block * NEAR_ROWS, (block + 1) * NEAR_ROWS)
        kn_s[near_rows, :] = nn(pool_near, key(block)).astype(BF16)
        vn_s[near_rows, :] = nn(pool_near, value(block)).astype(BF16)
    for pair in range(WIDE // 2):
        blocks = (2 * pair, 2 * pair + 1)
        befores = tuple(max(b - 1, 0) for b in blocks)
        qs, gs = [query(b) for b in blocks], [grad(b) for b in blocks]
        q, g = jnp.concatenate(qs, axis=0), jnp.concatenate(gs, axis=0)
        near = 2 * NEAR_ROWS * pair + NEAR_ROWS
        far_from = wide2 + near
        total = far_from + FAR_ALL
        halves = [slice(b * BLOCK, (b + 1) * BLOCK) for b in range(2)]
        for b, cols in enumerate(halves):
            if blocks[b] == 0:
                s_s[0:BLOCK, cols] = jnp.full((BLOCK, BLOCK), BLOCKED, F32)
            else:
                s_s[0:BLOCK, cols] = nt(key(befores[b]), qs[b])
            s_s[BLOCK:wide2, cols] = jnp.where(later, F32(BLOCKED), nt(key(blocks[b]), qs[b]))
        s_s[wide2:far_from, :] = nt(kn_s[0:near, :], q)
        s_s[far_from - NEAR_ROWS : far_from, 0:BLOCK] = jnp.full((NEAR_ROWS, BLOCK), BLOCKED, F32)
        for i in range(0, FAR_ALL, BLOCK):
            s_s[far_from + i : far_from + i + BLOCK, :] = nt(kf[i : i + BLOCK, :], q) + far_bias[i : i + BLOCK]
        chunks = [(0, BLOCK), (BLOCK, BLOCK)]
        chunks += [(wide2 + i, min(BLOCK, near - i)) for i in range(0, near, BLOCK)]
        chunks += [(far_from + i, BLOCK) for i in range(0, FAR_ALL, BLOCK)]
        top = None
        for start, size in chunks:
            here = jnp.max(s_s[start : start + size, :].reshape(size // 8, 8, wide2), axis=0)
            top = here if top is None else jnp.maximum(top, here)
        top = jnp.max(top, axis=0, keepdims=True)
        norm = None
        for start, size in chunks:
            e = jnp.exp2((s_s[start : start + size, :] - top) * exponent)
            s_s[start : start + size, :] = e
            here = jnp.sum(e.reshape(size // 8, 8, wide2), axis=0)
            norm = here if norm is None else norm + here
        inverse = 1.0 / jnp.sum(norm, axis=0, keepdims=True)
        for start, size in chunks:
            e = s_s[start : start + size, :] * inverse
            s_s[start : start + size, :] = e
            w_s[start : start + size, :] = e.astype(BF16)
        sides = [
            tn(value(befores[b]), w_s[0:BLOCK, cols]) + tn(value(blocks[b]), w_s[BLOCK:wide2, cols])
            for b, cols in enumerate(halves)
        ]
        attended = jnp.concatenate(sides, axis=1)
        attended += tn(vn_s[0:near, :], w_s[wide2:far_from, :])
        attended += tn(vf, w_s[far_from:total, :])
        attended = attended.astype(BF16).astype(F32)
        q_rows = slice(pair * wide2, (pair + 1) * wide2)
        o_s[q_rows, :] = attended.T.astype(BF16)
        row_dot = jnp.sum(g.astype(F32).T * attended, axis=0, keepdims=True)

        def put(start, size, cols, dprob, dot):
            d_s[start : start + size, cols] = (s_s[start : start + size, cols] * (dprob - dot)).astype(BF16)

        every = slice(0, wide2)
        for b, cols in enumerate(halves):
            put(0, BLOCK, cols, nt(value(befores[b]), gs[b]), row_dot[:, cols])
            put(BLOCK, BLOCK, cols, nt(value(blocks[b]), gs[b]), row_dot[:, cols])
        put(wide2, near, every, nt(vn_s[0:near, :], g), row_dot)
        for i in range(0, FAR_ALL, BLOCK):
            put(far_from + i, BLOCK, every, nt(vf[i : i + BLOCK, :], g), row_dot)
        sides = []
        for b, cols in enumerate(halves):
            before, own = (slice(at * BLOCK, (at + 1) * BLOCK) for at in (befores[b], blocks[b]))
            sides.append(tn(key(befores[b]), d_s[0:BLOCK, cols]) + tn(key(blocks[b]), d_s[BLOCK:wide2, cols]))
            if blocks[b] > 0:
                dk_s[before, :] += nn(d_s[0:BLOCK, cols], qs[b])
                dv_s[before, :] += nn(w_s[0:BLOCK, cols], gs[b])
            dk_s[own, :] += nn(d_s[BLOCK:wide2, cols], qs[b])
            dv_s[own, :] += nn(w_s[BLOCK:wide2, cols], gs[b])
        grad_query = jnp.concatenate(sides, axis=1)
        grad_query += tn(kn_s[0:near, :], d_s[wide2:far_from, :])
        grad_query += tn(kf, d_s[far_from:total, :])
        dq_s[q_rows, :] = (grad_query * SCALE).T.astype(BF16)
        dkn_s[0:near, :] += nn(d_s[wide2:far_from, :], q)
        dvn_s[0:near, :] += nn(w_s[wide2:far_from, :], g)
        dkf_s[...] += nn(d_s[far_from:total, :], q)
        dvf_s[...] += nn(w_s[far_from:total, :], g)

    mine = slice(0, HEAD_DIM)
    if head:
        far_out[:, :, mine] = other_far[...]
        mine = slice(HEAD_DIM, PAIR)
    far_out[:, :SPAN_FAR, mine] = (dkf_s[...] * SCALE).astype(BF16).reshape(NARROW, SPAN_FAR, HEAD_DIM)
    far_out[:, SPAN_FAR:, mine] = dvf_s[...].astype(BF16).reshape(NARROW, SPAN_FAR, HEAD_DIM)
    for block in range(WIDE):
        rows = slice(block * BLOCK, (block + 1) * BLOCK)
        near_rows = slice(block * NEAR_ROWS, (block + 1) * NEAR_ROWS)
        dk_s[rows, :] = (dk_s[rows, :] + nn(spread_near, dkn_s[near_rows, :].astype(BF16))) * SCALE
        dv_s[rows, :] = dv_s[rows, :] + nn(spread_near, dvn_s[near_rows, :].astype(BF16))
    for part, chip in enumerate(CHIPS):
        for core in range(2):
            rows = pl.ds(pl.multiple_of(target(wide_at, (chip, core)) * BLOCK, BLOCK), BLOCK)
            for i, ref in enumerate((o_s, dq_s, dk_s, dv_s)):
                row = core * HALF + i * BLOCK
                outs[part][row : row + BLOCK, :] = ref[rows, :].astype(BF16)


def attend(head, at, parts, swapped, far, other_far=()):
    n = len(CHIPS)
    vmem, some = pl.BlockSpec(memory_space=pltpu.VMEM), pl.BlockSpec(memory_space=pl.ANY)
    rows = lambda count, kind: pltpu.VMEM((count, HEAD_DIM), kind)
    lists = lambda kind: pltpu.VMEM((SPAN, 2 * BLOCK), kind)
    outs = pl.pallas_call(
        functools.partial(attend_kernel, head),
        out_shape=[jax.ShapeDtypeStruct((2 * HALF, HEAD_DIM), BF16)] * n
        + [jax.ShapeDtypeStruct((NARROW, 2 * SPAN_FAR, (1 + head) * HEAD_DIM), BF16)],
        in_specs=[pl.BlockSpec(memory_space=pltpu.SMEM)] + [some] * (n + 1) + [vmem] * (1 + len(other_far)),
        out_specs=[vmem] * (n + 1),
        scratch_shapes=[pltpu.VMEM((WIDE, HALF, HEAD_DIM), BF16)]
        + [rows(SPAN_NEAR, BF16)] * 2 + [rows(SPAN, BF16)] * 2 + [rows(SPAN, F32)] * 2
        + [rows(SPAN_NEAR, F32)] * 2 + [rows(FAR_ALL, F32)] * 2
        + [lists(F32), lists(BF16), lists(BF16), pltpu.SemaphoreType.DMA((WIDE,))],
        compiler_params=pltpu.CompilerParams(vmem_limit_bytes=16 << 20),
        cost_estimate=pl.CostEstimate(flops=1_600_000_000, bytes_accessed=2 << 20, transcendentals=1 << 20),
        name=f"attend{head}",
    )(at, *parts, swapped, far, *other_far)
    return outs[:n], outs[n]


def total_kernel(at_ref, terms_ref, *outs):
    wide_at = at_ref[0]
    total = jnp.sum(terms_ref[...].astype(F32), axis=0).astype(BF16)
    shape = (TAIL, 2 * SPAN_FAR)
    row, column = lax.broadcasted_iota(jnp.int32, shape, 0), lax.broadcasted_iota(jnp.int32, shape, 1)
    for part, chip in enumerate(CHIPS):
        for core in range(2):
            first = target(wide_at, (chip, core)) * FAR_ROWS
            wanted = (row // FAR_ROWS) * SPAN_FAR + first + row % FAR_ROWS
            choose = jnp.where((column == wanted) & (row < 2 * FAR_ROWS), F32(1.0), F32(0.0)).astype(BF16)
            rows = nn(choose, total).astype(BF16)
            for head in range(2):
                at = (2 * core + head) * TAIL
                outs[part][at : at + TAIL, :] = rows[:, head * HEAD_DIM : (head + 1) * HEAD_DIM]


def total(at, terms):
    n = len(CHIPS)
    vmem = pl.BlockSpec(memory_space=pltpu.VMEM)
    return pl.pallas_call(
        total_kernel,
        out_shape=[jax.ShapeDtypeStruct((4 * TAIL, HEAD_DIM), BF16)] * n,
        in_specs=[pl.BlockSpec(memory_space=pltpu.SMEM), vmem],
        out_specs=[vmem] * n,
        compiler_params=pltpu.CompilerParams(vmem_limit_bytes=4 << 20),
        name="total",
    )(at, terms)


def unpack_kernel(at_ref, *refs):
    n = len(CHIPS)
    ins0, swapped0, ins1, swapped1 = refs[:n], refs[n], refs[n + 1 : 2 * n + 1], refs[2 * n + 1]
    tails, outs = refs[2 * n + 2 : 3 * n + 2], refs[3 * n + 2 : 3 * n + 6]
    held, far_s, sums, sems, far_sems = refs[3 * n + 6 :]
    wide_at = at_ref[0]
    pairs = arrivals(ins0, swapped0, lambda i: held.at[i])
    pairs += arrivals(ins1, swapped1, lambda i: held.at[WIDE + i])
    copies = copy_all(pairs, sems)
    rows = 2 * TAIL
    pairs = [(tails[i].at[pl.ds(0, rows), :], far_s.at[i]) for i in range(n)]
    pairs += [(swapped1.at[pl.ds(n * HALF + i * rows, rows), :], far_s.at[n + i]) for i in range(n)]
    for copy in copy_all(pairs, far_sems):
        copy.wait()
    for head in range(2):
        for part, step in enumerate(STEPS):
            copies[head * WIDE + part].wait()
            block = source(wide_at, step)
            columns = pl.ds(pl.multiple_of(block * PAIR + head * HEAD_DIM, HEAD_DIM), HEAD_DIM)
            far = far_s[part, head * TAIL : (head + 1) * TAIL, :].astype(F32) * (1.0 / FAR)
            for i in range(4):
                piece = held[head * WIDE + part, i * BLOCK : (i + 1) * BLOCK, :]
                if i >= 2:
                    terms = piece.astype(F32)
                    at = (i - 2) * FAR_ROWS
                    both = [terms[r * FAR : (r + 1) * FAR] + far[at + r : at + r + 1] for r in range(FAR_ROWS)]
                    piece = jnp.concatenate(both, axis=0).astype(BF16)
                sums[i, :, columns] = piece
    strip = BLOCK // 2
    pairs = []
    for i in range(4):
        for r in range(0, BLOCK, strip):
            pairs.append((sums.at[i, r : r + strip, :], outs[i].at[r : r + strip, :]))
    for copy in copy_all(pairs, sems):
        copy.wait()


def unpack(at, parts0, swapped0, parts1, swapped1, tails):
    n = len(CHIPS)
    some = pl.BlockSpec(memory_space=pl.ANY)
    return pl.pallas_call(
        unpack_kernel,
        out_shape=[jax.ShapeDtypeStruct((BLOCK, FEAT), BF16)] * 4,
        in_specs=[pl.BlockSpec(memory_space=pltpu.SMEM)] + [some] * (3 * n + 2),
        out_specs=[some] * 4,
        scratch_shapes=[
            pltpu.VMEM((2 * WIDE, HALF, HEAD_DIM), BF16),
            pltpu.VMEM((WIDE, 2 * TAIL, HEAD_DIM), BF16),
            pltpu.VMEM((4, BLOCK, FEAT), BF16),
            pltpu.SemaphoreType.DMA((2 * WIDE,)),
            pltpu.SemaphoreType.DMA((WIDE,)),
        ],
        compiler_params=pltpu.CompilerParams(vmem_limit_bytes=8 << 20),
        name="unpack",
    )(at, *parts0, swapped0, *parts1, swapped1, *tails)


def shards(queries, keys, values, grad_out):
    at = jnp.stack([lax.axis_index("wide"), lax.axis_index("narrow")]).astype(jnp.int32)
    parts0, parts1 = pack(at, queries, keys, values, grad_out)
    parts0 = to_chips(parts0)
    parts1, parts0 = after(parts1, parts0)
    parts1 = to_chips(parts1)
    swapped0 = to_other_core(parts0)
    far = lax.all_to_all(collect(at, parts0, swapped0), "narrow", 0, 0, tiled=True)
    out0, terms0 = attend(0, at, parts0, swapped0, far)
    parts1, own = after(parts1, out0[SENT:])
    out0 = [*out0[:SENT], *own]
    out1, terms = attend(1, at, parts1, to_other_core(parts1), far, (terms0,))
    out0 = to_chips(out0)
    swapped0 = to_other_core(out0)
    out1, (swapped0,) = after(out1, [swapped0])
    out1 = to_chips(out1)
    tails = to_chips(total(at, lax.all_to_all(terms, "narrow", 0, 0, tiled=True)))
    return tuple(unpack(at, out0, swapped0, out1, to_other_core([*out1, *tails]), tails))


def solution(mesh):
    rows = P(("narrow", "wide"), None)
    return jax.shard_map(
        shards, mesh=mesh, in_specs=(rows,) * 4, out_specs=(rows,) * 4, check_vma=False
    )
```

```python
import functools

import jax
import jax.numpy as jnp
from jax import lax
from jax.experimental import pallas as pl
from jax.experimental.pallas import tpu as pltpu
from jax.sharding import PartitionSpec as P

HEAD_DIM = 128
BLOCK = 128
NEAR = 4
FAR = 64
NEAR_ROWS = 32
FAR_ROWS = 2
WIDE = 8
NARROW = 32
SPAN = WIDE * BLOCK
SPAN_NEAR = WIDE * NEAR_ROWS
SPAN_FAR = WIDE * FAR_ROWS
FAR_ALL = NARROW * SPAN_FAR
FEAT = 2048
PAIR = 2 * HEAD_DIM
SCALE = HEAD_DIM**-0.5
LOG2E = 1.4426950408889634
BLOCKED = -1e30
F32 = jnp.float32
BF16 = jnp.bfloat16

CHIPS = [1, 3, 2, 0]
SENT = len(CHIPS) - 1
PART = 8 * BLOCK
TAIL = 16
STEPS = [(chip, core) for core in range(2) for chip in CHIPS]


def target(at, step):
    chip, core = step
    return ((at // 2 + chip) % 4) * 2 + (at % 2 + core) % 2


def source(at, step):
    chip, core = step
    return ((at // 2 + 4 - chip) % 4) * 2 + (at % 2 + core) % 2


def move(buffer, step):
    return lax.ppermute(buffer, "wide", [(s, target(s, step)) for s in range(WIDE)])


def to_chips(parts):
    return [move(part, (chip, 0)) for part, chip in zip(parts[:SENT], CHIPS)] + [parts[SENT]]


def to_chips_in_turn(parts):
    sides = [move(part, (chip, 0)) for part, chip in zip(parts[:2], CHIPS)]
    *sides, across = lax.optimization_barrier((*sides, parts[2]))
    return [*sides, move(across, (CHIPS[2], 0)), parts[SENT]]


def to_other_core(parts):
    return move(gather_halves(parts), (0, 1))


def copy_all(pairs, sems):
    copies = [pltpu.make_async_copy(src, dst, sems.at[i]) for i, (src, dst) in enumerate(pairs)]
    for copy in copies:
        copy.start()
    return copies


def gather_kernel(*refs):
    n = len(refs) - 2
    ins, out, sems = refs[:n], refs[n], refs[n + 1]
    pairs, row = [], 0
    for ref in ins:
        half = ref.shape[0] // 2
        pairs.append((ref.at[pl.ds(half, half), :], out.at[pl.ds(row, half), :]))
        row += half
    for copy in copy_all(pairs, sems):
        copy.wait()


def gather_halves(parts):
    n = len(parts)
    some = pl.BlockSpec(memory_space=pl.ANY)
    return pl.pallas_call(
        gather_kernel,
        out_shape=jax.ShapeDtypeStruct((sum(part.shape[0] for part in parts) // 2, HEAD_DIM), BF16),
        in_specs=[some] * n,
        out_specs=some,
        scratch_shapes=[pltpu.SemaphoreType.DMA((n,))],
        compiler_params=pltpu.CompilerParams(vmem_limit_bytes=1 << 20),
        name="gather_halves",
    )(*parts)


def nt(a, b):
    return lax.dot_general(a, b, (((1,), (1,)), ((), ())), preferred_element_type=F32)


def nn(a, b):
    return lax.dot_general(a, b, (((1,), (0,)), ((), ())), preferred_element_type=F32)


def tn(a, b):
    return lax.dot_general(a, b, (((0,), (0,)), ((), ())), preferred_element_type=F32)


def pooling(rows, factor):
    shape = (rows, rows * factor)
    group = lax.broadcasted_iota(jnp.int32, shape, 1) // factor
    member = group == lax.broadcasted_iota(jnp.int32, shape, 0)
    return jnp.where(member, F32(1.0 / factor), F32(0.0)).astype(BF16)


def spreading(rows, factor):
    shape = (rows * factor, rows)
    group = lax.broadcasted_iota(jnp.int32, shape, 0) // factor
    member = group == lax.broadcasted_iota(jnp.int32, shape, 1)
    return jnp.where(member, F32(1.0 / factor), F32(0.0)).astype(BF16)


def tail_kernel(at_ref, k_ref, v_ref, *refs):
    n = len(CHIPS)
    tails, (held, far_s, sems) = refs[:n], refs[n:]
    wide_at = at_ref[0]
    strip = BLOCK // 4
    pairs = []
    for i, ref in enumerate((k_ref, v_ref)):
        for r in range(0, BLOCK, strip):
            pairs.append((ref.at[r : r + strip, :], held.at[i, r : r + strip, :]))
    for copy in copy_all(pairs, sems):
        copy.wait()
    pool_near = pooling(NEAR_ROWS, NEAR)
    group = lax.broadcasted_iota(jnp.int32, (TAIL, NEAR_ROWS), 1) // (FAR // NEAR)
    row = lax.broadcasted_iota(jnp.int32, (TAIL, NEAR_ROWS), 0)
    far = None
    for i in range(2):
        near = nn(pool_near, held[i]).astype(BF16)
        pool_far = jnp.where(row == group + i * FAR_ROWS, F32(NEAR / FAR), F32(0.0)).astype(BF16)
        far = nn(pool_far, near) if far is None else far + nn(pool_far, near)
    far_s[...] = far.astype(BF16)
    for part, chip in enumerate(CHIPS):
        for core in range(2):
            for head in range(2):
                column = target(wide_at, (chip, core)) * PAIR + head * HEAD_DIM
                row = (2 * core + head) * TAIL
                tails[part][row : row + TAIL, :] = far_s[:, pl.ds(pl.multiple_of(column, HEAD_DIM), HEAD_DIM)]


def tails_of(at, keys, values):
    n = len(CHIPS)
    some = pl.BlockSpec(memory_space=pl.ANY)
    return pl.pallas_call(
        tail_kernel,
        out_shape=[jax.ShapeDtypeStruct((4 * TAIL, HEAD_DIM), BF16)] * n,
        in_specs=[pl.BlockSpec(memory_space=pltpu.SMEM)] + [some] * 2,
        out_specs=[pl.BlockSpec(memory_space=pltpu.VMEM)] * n,
        scratch_shapes=[
            pltpu.VMEM((2, BLOCK, FEAT), BF16),
            pltpu.VMEM((TAIL, FEAT), BF16),
            pltpu.SemaphoreType.DMA((8,)),
        ],
        compiler_params=pltpu.CompilerParams(vmem_limit_bytes=58 << 20),
        name="tails_of",
    )(at, keys, values)


def pack_kernel(at_ref, k_ref, v_ref, q_ref, g_ref, *refs):
    n = len(CHIPS)
    outs, (held, staged, in_sems, out_sems) = refs[:n], refs[n:]
    wide_at = at_ref[0]
    strip = BLOCK // 4
    pairs = []
    for i, ref in enumerate((k_ref, v_ref, q_ref, g_ref)):
        for r in range(0, BLOCK, strip):
            pairs.append((ref.at[r : r + strip, :], held.at[i, r : r + strip, :]))
    for copy in copy_all(pairs, in_sems):
        copy.wait()
    last = []
    for part, chip in enumerate(CHIPS):
        for core in range(2):
            for head in range(2):
                column = target(wide_at, (chip, core)) * PAIR + head * HEAD_DIM
                columns = pl.ds(pl.multiple_of(column, HEAD_DIM), HEAD_DIM)
                for i in range(4):
                    row = core * PART + (2 * i + head) * BLOCK
                    staged[part, row : row + BLOCK, :] = held[i, :, columns]
        last.append(pltpu.make_async_copy(staged.at[part], outs[part], out_sems.at[part]))
        last[-1].start()
    for copy in last:
        copy.wait()


def pack(at, queries, keys, values, grad_out):
    n = len(CHIPS)
    part = jax.ShapeDtypeStruct((2 * PART, HEAD_DIM), BF16)
    some = pl.BlockSpec(memory_space=pl.ANY)
    return pl.pallas_call(
        pack_kernel,
        out_shape=[part] * n,
        in_specs=[pl.BlockSpec(memory_space=pltpu.SMEM)] + [some] * 4,
        out_specs=[some] * n,
        scratch_shapes=[
            pltpu.VMEM((4, BLOCK, FEAT), BF16),
            pltpu.VMEM((n, *part.shape), BF16),
            pltpu.SemaphoreType.DMA((16,)),
            pltpu.SemaphoreType.DMA((n,)),
        ],
        compiler_params=pltpu.CompilerParams(vmem_limit_bytes=58 << 20),
        cost_estimate=pl.CostEstimate(flops=0, bytes_accessed=4 << 20, transcendentals=0),
        name="pack",
    )(at, keys, values, queries, grad_out)


def arrivals(parts, swapped, place, start=0, rows=PART):
    n = len(CHIPS)
    half = parts[0].shape[0] // 2
    pairs = [(parts[i].at[pl.ds(start, rows), :], place(i)) for i in range(n)]
    return pairs + [(swapped.at[pl.ds(i * half + start, rows), :], place(n + i)) for i in range(n)]


def collect_kernel(at_ref, *refs):
    n = len(CHIPS)
    ins, swapped, out, held, sems = refs[:n], refs[n], refs[n + 1], refs[n + 2], refs[n + 3]
    wide_at = at_ref[0]
    pairs = []
    for head in range(2):
        place = lambda i: held.at[head, source(wide_at, STEPS[i])]
        pairs += arrivals(ins, swapped, place, head * TAIL, TAIL)
    for copy in copy_all(pairs, sems):
        copy.wait()
    shape = (2 * SPAN_FAR, WIDE * TAIL)
    row, column = lax.broadcasted_iota(jnp.int32, shape, 0), lax.broadcasted_iota(jnp.int32, shape, 1)
    inner = row % SPAN_FAR
    wanted = (inner // FAR_ROWS) * TAIL + inner % FAR_ROWS + (row // SPAN_FAR) * FAR_ROWS
    choose = jnp.where(column == wanted, F32(1.0), F32(0.0)).astype(BF16)
    for head in range(2):
        rows = nn(choose, held[head].reshape(WIDE * TAIL, HEAD_DIM)).astype(BF16)
        lanes = slice(head * HEAD_DIM, (head + 1) * HEAD_DIM)
        out[:, :, lanes] = jnp.broadcast_to(rows[None], (NARROW, 2 * SPAN_FAR, HEAD_DIM))


def collect(at, parts, swapped):
    n = len(CHIPS)
    return pl.pallas_call(
        collect_kernel,
        out_shape=jax.ShapeDtypeStruct((NARROW, 2 * SPAN_FAR, PAIR), BF16),
        in_specs=[pl.BlockSpec(memory_space=pltpu.SMEM)] + [pl.BlockSpec(memory_space=pl.ANY)] * (n + 1),
        out_specs=pl.BlockSpec(memory_space=pltpu.VMEM),
        scratch_shapes=[pltpu.VMEM((2, WIDE, TAIL, HEAD_DIM), BF16), pltpu.SemaphoreType.DMA((2 * WIDE,))],
        compiler_params=pltpu.CompilerParams(vmem_limit_bytes=4 << 20),
        name="collect",
    )(at, *parts, swapped)


def attend_kernel(at_ref, *refs):
    n = len(CHIPS)
    ins, swapped, far_ref, outs, far_out = refs[:n], refs[n], refs[n + 1], refs[n + 2 : 2 * n + 2], refs[2 * n + 2]
    held, kn_s, vn_s, o_s, dq_s, dk_s, dv_s, dkn_s, dvn_s, dkf_s, dvf_s, s_s, w_s, d_s, sems = refs[2 * n + 3 :]
    wide_at = at_ref[0]
    far_seen = at_ref[1] * SPAN_FAR
    copies = copy_all(arrivals(ins, swapped, lambda i: held.at[source(wide_at, STEPS[i])]), sems)
    for ref in (dk_s, dv_s, dkn_s, dvn_s, dkf_s, dvf_s):
        ref[...] = jnp.zeros(ref.shape, F32)
    for copy in copies:
        copy.wait()
    pool_near = pooling(NEAR_ROWS, NEAR)
    spread_near = spreading(NEAR_ROWS, NEAR)
    later = lax.broadcasted_iota(jnp.int32, (BLOCK, BLOCK), 0) > lax.broadcasted_iota(
        jnp.int32, (BLOCK, BLOCK), 1
    )
    far_blocked = lax.broadcasted_iota(jnp.int32, (FAR_ALL, 1), 0) >= far_seen
    far_bias = jnp.where(far_blocked, F32(BLOCKED), F32(0.0))
    exponent = SCALE * LOG2E
    wide2 = 2 * BLOCK
    for head in range(2):
        lanes = slice(head * HEAD_DIM, (head + 1) * HEAD_DIM)
        kf = far_ref[:, :SPAN_FAR, lanes].reshape(FAR_ALL, HEAD_DIM)
        vf = far_ref[:, SPAN_FAR:, lanes].reshape(FAR_ALL, HEAD_DIM)

        def rows_of(array, block):
            row = (2 * array + head) * BLOCK
            return held[block, row : row + BLOCK, :]

        key = functools.partial(rows_of, 0)
        value = functools.partial(rows_of, 1)
        query = functools.partial(rows_of, 2)
        grad = functools.partial(rows_of, 3)
        for block in range(WIDE):
            near_rows = slice(block * NEAR_ROWS, (block + 1) * NEAR_ROWS)
            kn_s[head, near_rows, :] = nn(pool_near, key(block)).astype(BF16)
            vn_s[head, near_rows, :] = nn(pool_near, value(block)).astype(BF16)
        for pair in range(WIDE // 2):
            blocks = (2 * pair, 2 * pair + 1)
            befores = tuple(max(b - 1, 0) for b in blocks)
            qs, gs = [query(b) for b in blocks], [grad(b) for b in blocks]
            q, g = jnp.concatenate(qs, axis=0), jnp.concatenate(gs, axis=0)
            near = 2 * NEAR_ROWS * pair + NEAR_ROWS
            far_from = wide2 + near
            total = far_from + FAR_ALL
            halves = [slice(b * BLOCK, (b + 1) * BLOCK) for b in range(2)]
            for b, cols in enumerate(halves):
                if blocks[b] == 0:
                    s_s[0:BLOCK, cols] = jnp.full((BLOCK, BLOCK), BLOCKED, F32)
                else:
                    s_s[0:BLOCK, cols] = nt(key(befores[b]), qs[b])
                s_s[BLOCK:wide2, cols] = jnp.where(later, F32(BLOCKED), nt(key(blocks[b]), qs[b]))
            s_s[wide2:far_from, :] = nt(kn_s[head, 0:near, :], q)
            s_s[far_from - NEAR_ROWS : far_from, 0:BLOCK] = jnp.full((NEAR_ROWS, BLOCK), BLOCKED, F32)
            for i in range(0, FAR_ALL, BLOCK):
                s_s[far_from + i : far_from + i + BLOCK, :] = nt(kf[i : i + BLOCK, :], q) + far_bias[i : i + BLOCK]
            chunks = [(0, BLOCK), (BLOCK, BLOCK)]
            chunks += [(wide2 + i, min(BLOCK, near - i)) for i in range(0, near, BLOCK)]
            chunks += [(far_from + i, BLOCK) for i in range(0, FAR_ALL, BLOCK)]
            top = None
            for start, size in chunks:
                here = jnp.max(s_s[start : start + size, :].reshape(size // 8, 8, wide2), axis=0)
                top = here if top is None else jnp.maximum(top, here)
            top = jnp.max(top, axis=0, keepdims=True)
            norm = None
            for start, size in chunks:
                e = jnp.exp2((s_s[start : start + size, :] - top) * exponent)
                w_s[start : start + size, :] = e.astype(BF16)
                here = jnp.sum(e.reshape(size // 8, 8, wide2), axis=0)
                norm = here if norm is None else norm + here
            inverse = 1.0 / jnp.sum(norm, axis=0, keepdims=True)
            sides = [
                tn(value(befores[b]), w_s[0:BLOCK, cols]) + tn(value(blocks[b]), w_s[BLOCK:wide2, cols])
                for b, cols in enumerate(halves)
            ]
            attended = jnp.concatenate(sides, axis=1)
            attended += tn(vn_s[head, 0:near, :], w_s[wide2:far_from, :])
            attended += tn(vf, w_s[far_from:total, :])
            attended = (attended * inverse).astype(BF16).astype(F32)
            q_rows = slice(pair * wide2, (pair + 1) * wide2)
            o_s[head, q_rows, :] = attended.T.astype(BF16)
            grad_t = g.astype(F32).T
            row_dot = jnp.sum(grad_t * attended, axis=0, keepdims=True) * inverse
            g = (grad_t * inverse).T.astype(BF16)
            gs = [g[cols] for cols in halves]

            def put(start, size, cols, dprob, dot):
                d_s[start : start + size, cols] = (w_s[start : start + size, cols].astype(F32) * (dprob - dot)).astype(BF16)

            every = slice(0, wide2)
            for b, cols in enumerate(halves):
                put(0, BLOCK, cols, nt(value(befores[b]), gs[b]), row_dot[:, cols])
                put(BLOCK, BLOCK, cols, nt(value(blocks[b]), gs[b]), row_dot[:, cols])
            put(wide2, near, every, nt(vn_s[head, 0:near, :], g), row_dot)
            for i in range(0, FAR_ALL, BLOCK):
                put(far_from + i, BLOCK, every, nt(vf[i : i + BLOCK, :], g), row_dot)
            sides = []
            for b, cols in enumerate(halves):
                before, own = (slice(at * BLOCK, (at + 1) * BLOCK) for at in (befores[b], blocks[b]))
                sides.append(tn(key(befores[b]), d_s[0:BLOCK, cols]) + tn(key(blocks[b]), d_s[BLOCK:wide2, cols]))
                if blocks[b] > 0:
                    dk_s[head, before, :] += nn(d_s[0:BLOCK, cols], qs[b])
                    dv_s[head, before, :] += nn(w_s[0:BLOCK, cols], gs[b])
                dk_s[head, own, :] += nn(d_s[BLOCK:wide2, cols], qs[b])
                dv_s[head, own, :] += nn(w_s[BLOCK:wide2, cols], gs[b])
            grad_query = jnp.concatenate(sides, axis=1)
            grad_query += tn(kn_s[head, 0:near, :], d_s[wide2:far_from, :])
            grad_query += tn(kf, d_s[far_from:total, :])
            dq_s[head, q_rows, :] = (grad_query * SCALE).T.astype(BF16)
            dkn_s[head, 0:near, :] += nn(d_s[wide2:far_from, :], q)
            dvn_s[head, 0:near, :] += nn(w_s[wide2:far_from, :], g)
            dkf_s[head] += nn(d_s[far_from:total, :], q)
            dvf_s[head] += nn(w_s[far_from:total, :], g)

        far_out[:, :SPAN_FAR, lanes] = (dkf_s[head] * SCALE).astype(BF16).reshape(NARROW, SPAN_FAR, HEAD_DIM)
        far_out[:, SPAN_FAR:, lanes] = dvf_s[head].astype(BF16).reshape(NARROW, SPAN_FAR, HEAD_DIM)
        for block in range(WIDE):
            rows = slice(block * BLOCK, (block + 1) * BLOCK)
            near_rows = slice(block * NEAR_ROWS, (block + 1) * NEAR_ROWS)
            dk_s[head, rows, :] = (dk_s[head, rows, :] + nn(spread_near, dkn_s[head, near_rows, :].astype(BF16))) * SCALE
            dv_s[head, rows, :] = dv_s[head, rows, :] + nn(spread_near, dvn_s[head, near_rows, :].astype(BF16))
        for part, chip in enumerate(CHIPS):
            for core in range(2):
                rows = pl.ds(pl.multiple_of(target(wide_at, (chip, core)) * BLOCK, BLOCK), BLOCK)
                for i, ref in enumerate((o_s, dq_s, dk_s, dv_s)):
                    row = core * PART + (2 * i + head) * BLOCK
                    outs[part][row : row + BLOCK, :] = ref[head, rows, :].astype(BF16)


def attend(at, parts, swapped, far):
    n = len(CHIPS)
    vmem, some = pl.BlockSpec(memory_space=pltpu.VMEM), pl.BlockSpec(memory_space=pl.ANY)
    both = lambda rows, kind: pltpu.VMEM((2, rows, HEAD_DIM), kind)
    lists = lambda kind: pltpu.VMEM((SPAN, 2 * BLOCK), kind)
    outs = pl.pallas_call(
        attend_kernel,
        out_shape=[jax.ShapeDtypeStruct((2 * PART, HEAD_DIM), BF16)] * n
        + [jax.ShapeDtypeStruct((NARROW, 2 * SPAN_FAR, PAIR), BF16)],
        in_specs=[pl.BlockSpec(memory_space=pltpu.SMEM)] + [some] * (n + 1) + [vmem],
        out_specs=[vmem] * (n + 1),
        scratch_shapes=[pltpu.VMEM((WIDE, PART, HEAD_DIM), BF16)]
        + [both(SPAN_NEAR, BF16)] * 2 + [both(SPAN, BF16)] * 2 + [both(SPAN, F32)] * 2
        + [both(SPAN_NEAR, F32)] * 2 + [both(FAR_ALL, F32)] * 2
        + [lists(F32), lists(BF16), lists(BF16), pltpu.SemaphoreType.DMA((WIDE,))],
        compiler_params=pltpu.CompilerParams(vmem_limit_bytes=20 << 20),
        cost_estimate=pl.CostEstimate(flops=3_200_000_000, bytes_accessed=4 << 20, transcendentals=2 << 20),
        name="attend",
    )(at, *parts, swapped, far)
    return outs[:n], outs[n]


def total_kernel(at_ref, terms_ref, *outs):
    wide_at = at_ref[0]
    total = jnp.sum(terms_ref[...].astype(F32), axis=0).astype(BF16)
    shape = (TAIL, 2 * SPAN_FAR)
    row, column = lax.broadcasted_iota(jnp.int32, shape, 0), lax.broadcasted_iota(jnp.int32, shape, 1)
    for part, chip in enumerate(CHIPS):
        for core in range(2):
            first = target(wide_at, (chip, core)) * FAR_ROWS
            wanted = (row // FAR_ROWS) * SPAN_FAR + first + row % FAR_ROWS
            choose = jnp.where((column == wanted) & (row < 2 * FAR_ROWS), F32(1.0), F32(0.0)).astype(BF16)
            rows = nn(choose, total).astype(BF16)
            for head in range(2):
                at = (2 * core + head) * TAIL
                outs[part][at : at + TAIL, :] = rows[:, head * HEAD_DIM : (head + 1) * HEAD_DIM]


def total(at, terms):
    n = len(CHIPS)
    vmem = pl.BlockSpec(memory_space=pltpu.VMEM)
    return pl.pallas_call(
        total_kernel,
        out_shape=[jax.ShapeDtypeStruct((4 * TAIL, HEAD_DIM), BF16)] * n,
        in_specs=[pl.BlockSpec(memory_space=pltpu.SMEM), vmem],
        out_specs=[vmem] * n,
        compiler_params=pltpu.CompilerParams(vmem_limit_bytes=4 << 20),
        name="total",
    )(at, terms)


def unpack_kernel(at_ref, *refs):
    n = len(CHIPS)
    ins, swapped, tails, outs = refs[:n], refs[n], refs[n + 1 : 2 * n + 1], refs[2 * n + 1 : 2 * n + 5]
    held, far_s, sums, sems, far_sems, out_sems = refs[2 * n + 5 :]
    wide_at = at_ref[0]
    copies = copy_all(arrivals(ins, swapped, lambda i: held.at[i]), sems)
    rows = 2 * TAIL
    pairs = [(tails[i].at[pl.ds(0, rows), :], far_s.at[i]) for i in range(n)]
    pairs += [(swapped.at[pl.ds(n * PART + i * rows, rows), :], far_s.at[n + i]) for i in range(n)]
    for copy in copy_all(pairs, far_sems):
        copy.wait()
    for part, step in enumerate(STEPS):
        copies[part].wait()
        block = source(wide_at, step)
        for head in range(2):
            columns = pl.ds(pl.multiple_of(block * PAIR + head * HEAD_DIM, HEAD_DIM), HEAD_DIM)
            far = far_s[part, head * TAIL : (head + 1) * TAIL, :].astype(F32) * (1.0 / FAR)
            for i in range(4):
                row = (2 * i + head) * BLOCK
                piece = held[part, row : row + BLOCK, :]
                if i >= 2:
                    terms = piece.astype(F32)
                    at = (i - 2) * FAR_ROWS
                    both = [terms[r * FAR : (r + 1) * FAR] + far[at + r : at + r + 1] for r in range(FAR_ROWS)]
                    piece = jnp.concatenate(both, axis=0).astype(BF16)
                sums[i, :, columns] = piece
    strip = BLOCK // 4
    pairs = []
    for i in range(4):
        for r in range(0, BLOCK, strip):
            pairs.append((sums.at[i, r : r + strip, :], outs[i].at[r : r + strip, :]))
    for copy in copy_all(pairs, out_sems):
        copy.wait()


def unpack(at, parts, swapped, tails):
    n = len(CHIPS)
    some = pl.BlockSpec(memory_space=pl.ANY)
    return pl.pallas_call(
        unpack_kernel,
        out_shape=[jax.ShapeDtypeStruct((BLOCK, FEAT), BF16)] * 4,
        in_specs=[pl.BlockSpec(memory_space=pltpu.SMEM)] + [some] * (2 * n + 1),
        out_specs=[some] * 4,
        scratch_shapes=[
            pltpu.VMEM((WIDE, PART, HEAD_DIM), BF16),
            pltpu.VMEM((WIDE, 2 * TAIL, HEAD_DIM), BF16),
            pltpu.VMEM((4, BLOCK, FEAT), BF16),
            pltpu.SemaphoreType.DMA((WIDE,)),
            pltpu.SemaphoreType.DMA((WIDE,)),
            pltpu.SemaphoreType.DMA((16,)),
        ],
        compiler_params=pltpu.CompilerParams(vmem_limit_bytes=8 << 20),
        name="unpack",
    )(at, *parts, swapped, *tails)


def shards(queries, keys, values, grad_out):
    at = jnp.stack([lax.axis_index("wide"), lax.axis_index("narrow")]).astype(jnp.int32)
    tails = to_chips(tails_of(at, keys, values))
    parts = pack(at, queries, keys, values, grad_out)
    tails, parts = lax.optimization_barrier((list(tails), list(parts)))
    swapped = to_other_core(tails)
    swapped, *parts = lax.optimization_barrier((swapped, *parts))
    parts = to_chips_in_turn(parts)
    far = lax.all_to_all(collect(at, tails, swapped), "narrow", 0, 0, tiled=True)
    far, *parts = lax.optimization_barrier((far, *parts))
    outs, terms = attend(at, parts, to_other_core(parts), far)
    outs = to_chips_in_turn(outs)
    tails = to_chips(total(at, lax.all_to_all(terms, "narrow", 0, 0, tiled=True)))
    return tuple(unpack(at, outs, to_other_core([*outs, *tails]), tails))


def solution(mesh):
    rows = P(("narrow", "wide"), None)
    return jax.shard_map(
        shards, mesh=mesh, in_specs=(rows,) * 4, out_specs=(rows,) * 4, check_vma=False
    )
```

```python
import functools

import jax
import jax.numpy as jnp
from jax import lax
from jax.experimental import pallas as pl
from jax.experimental.pallas import tpu as pltpu
from jax.sharding import PartitionSpec as P

HEAD_DIM = 128
BLOCK = 128
NEAR = 4
FAR = 64
NEAR_ROWS = 32
FAR_ROWS = 2
WIDE = 8
NARROW = 32
SPAN = WIDE * BLOCK
SPAN_NEAR = WIDE * NEAR_ROWS
SPAN_FAR = WIDE * FAR_ROWS
FAR_ALL = NARROW * SPAN_FAR
FEAT = 2048
PAIR = 2 * HEAD_DIM
SCALE = HEAD_DIM**-0.5
LOG2E = 1.4426950408889634
BLOCKED = -1e30
F32 = jnp.float32
BF16 = jnp.bfloat16

CHIPS = [1, 3, 2, 0]
SENT = len(CHIPS) - 1
PART = 8 * BLOCK
TAIL = 16
STEPS = [(chip, core) for core in range(2) for chip in CHIPS]


def target(at, step):
    chip, core = step
    return ((at // 2 + chip) % 4) * 2 + (at % 2 + core) % 2


def source(at, step):
    chip, core = step
    return ((at // 2 + 4 - chip) % 4) * 2 + (at % 2 + core) % 2


def move(buffer, step):
    return lax.ppermute(buffer, "wide", [(s, target(s, step)) for s in range(WIDE)])


def to_chips(parts):
    return [move(part, (chip, 0)) for part, chip in zip(parts[:SENT], CHIPS)] + [parts[SENT]]


def to_chips_in_turn(parts):
    sides = [move(part, (chip, 0)) for part, chip in zip(parts[:2], CHIPS)]
    *sides, across = lax.optimization_barrier((*sides, parts[2]))
    return [*sides, move(across, (CHIPS[2], 0)), parts[SENT]]


def to_other_core(parts):
    return move(gather_halves(parts), (0, 1))


def copy_all(pairs, sems):
    copies = [pltpu.make_async_copy(src, dst, sems.at[i]) for i, (src, dst) in enumerate(pairs)]
    for copy in copies:
        copy.start()
    return copies


def gather_kernel(*refs):
    n = len(refs) - 2
    ins, out, sems = refs[:n], refs[n], refs[n + 1]
    pairs, row = [], 0
    for ref in ins:
        half = ref.shape[0] // 2
        pairs.append((ref.at[pl.ds(half, half), :], out.at[pl.ds(row, half), :]))
        row += half
    for copy in copy_all(pairs, sems):
        copy.wait()


def gather_halves(parts):
    n = len(parts)
    some = pl.BlockSpec(memory_space=pl.ANY)
    return pl.pallas_call(
        gather_kernel,
        out_shape=jax.ShapeDtypeStruct((sum(part.shape[0] for part in parts) // 2, HEAD_DIM), BF16),
        in_specs=[some] * n,
        out_specs=some,
        scratch_shapes=[pltpu.SemaphoreType.DMA((n,))],
        compiler_params=pltpu.CompilerParams(vmem_limit_bytes=1 << 20),
        name="gather_halves",
    )(*parts)


def nt(a, b):
    return lax.dot_general(a, b, (((1,), (1,)), ((), ())), preferred_element_type=F32)


def nn(a, b):
    return lax.dot_general(a, b, (((1,), (0,)), ((), ())), preferred_element_type=F32)


def tn(a, b):
    return lax.dot_general(a, b, (((0,), (0,)), ((), ())), preferred_element_type=F32)


def pooling(rows, factor):
    shape = (rows, rows * factor)
    group = lax.broadcasted_iota(jnp.int32, shape, 1) // factor
    member = group == lax.broadcasted_iota(jnp.int32, shape, 0)
    return jnp.where(member, F32(1.0 / factor), F32(0.0)).astype(BF16)


def spreading(rows, factor):
    shape = (rows * factor, rows)
    group = lax.broadcasted_iota(jnp.int32, shape, 0) // factor
    member = group == lax.broadcasted_iota(jnp.int32, shape, 1)
    return jnp.where(member, F32(1.0 / factor), F32(0.0)).astype(BF16)


def tail_kernel(at_ref, k_ref, v_ref, *refs):
    n = len(CHIPS)
    tails, (held, far_s, sems) = refs[:n], refs[n:]
    wide_at = at_ref[0]
    strip = BLOCK // 4
    pairs = []
    for i, ref in enumerate((k_ref, v_ref)):
        for r in range(0, BLOCK, strip):
            pairs.append((ref.at[r : r + strip, :], held.at[i, r : r + strip, :]))
    copies = copy_all(pairs, sems)
    pool_near = pooling(NEAR_ROWS, NEAR)
    group = lax.broadcasted_iota(jnp.int32, (TAIL, NEAR_ROWS), 1) // (FAR // NEAR)
    row = lax.broadcasted_iota(jnp.int32, (TAIL, NEAR_ROWS), 0)
    far = None
    for i in range(2):
        for copy in copies[4 * i : 4 * i + 4]:
            copy.wait()
        near = nn(pool_near, held[i]).astype(BF16)
        pool_far = jnp.where(row == group + i * FAR_ROWS, F32(NEAR / FAR), F32(0.0)).astype(BF16)
        far = nn(pool_far, near) if far is None else far + nn(pool_far, near)
    far_s[...] = far.astype(BF16)
    for part, chip in enumerate(CHIPS):
        for core in range(2):
            for head in range(2):
                column = target(wide_at, (chip, core)) * PAIR + head * HEAD_DIM
                row = (2 * core + head) * TAIL
                tails[part][row : row + TAIL, :] = far_s[:, pl.ds(pl.multiple_of(column, HEAD_DIM), HEAD_DIM)]


def tails_of(at, keys, values):
    n = len(CHIPS)
    some = pl.BlockSpec(memory_space=pl.ANY)
    return pl.pallas_call(
        tail_kernel,
        out_shape=[jax.ShapeDtypeStruct((4 * TAIL, HEAD_DIM), BF16)] * n,
        in_specs=[pl.BlockSpec(memory_space=pltpu.SMEM)] + [some] * 2,
        out_specs=[pl.BlockSpec(memory_space=pltpu.VMEM)] * n,
        scratch_shapes=[
            pltpu.VMEM((2, BLOCK, FEAT), BF16),
            pltpu.VMEM((TAIL, FEAT), BF16),
            pltpu.SemaphoreType.DMA((8,)),
        ],
        compiler_params=pltpu.CompilerParams(vmem_limit_bytes=58 << 20),
        name="tails_of",
    )(at, keys, values)


def pack_kernel(at_ref, k_ref, v_ref, q_ref, g_ref, *refs):
    n = len(CHIPS)
    outs, (held, staged, in_sems, out_sems) = refs[:n], refs[n:]
    wide_at = at_ref[0]
    strip = BLOCK // 4
    pairs = []
    for i, ref in enumerate((k_ref, v_ref, q_ref, g_ref)):
        for r in range(0, BLOCK, strip):
            pairs.append((ref.at[r : r + strip, :], held.at[i, r : r + strip, :]))
    for copy in copy_all(pairs, in_sems):
        copy.wait()
    last = []
    for part, chip in enumerate(CHIPS):
        for core in range(2):
            for head in range(2):
                column = target(wide_at, (chip, core)) * PAIR + head * HEAD_DIM
                columns = pl.ds(pl.multiple_of(column, HEAD_DIM), HEAD_DIM)
                for i in range(4):
                    row = core * PART + (2 * i + head) * BLOCK
                    staged[part, row : row + BLOCK, :] = held[i, :, columns]
        last.append(pltpu.make_async_copy(staged.at[part], outs[part], out_sems.at[part]))
        last[-1].start()
    for copy in last:
        copy.wait()


def pack(at, queries, keys, values, grad_out):
    n = len(CHIPS)
    part = jax.ShapeDtypeStruct((2 * PART, HEAD_DIM), BF16)
    some = pl.BlockSpec(memory_space=pl.ANY)
    return pl.pallas_call(
        pack_kernel,
        out_shape=[part] * n,
        in_specs=[pl.BlockSpec(memory_space=pltpu.SMEM)] + [some] * 4,
        out_specs=[some] * n,
        scratch_shapes=[
            pltpu.VMEM((4, BLOCK, FEAT), BF16),
            pltpu.VMEM((n, *part.shape), BF16),
            pltpu.SemaphoreType.DMA((16,)),
            pltpu.SemaphoreType.DMA((n,)),
        ],
        compiler_params=pltpu.CompilerParams(vmem_limit_bytes=58 << 20),
        cost_estimate=pl.CostEstimate(flops=0, bytes_accessed=4 << 20, transcendentals=0),
        name="pack",
    )(at, keys, values, queries, grad_out)


def arrivals(parts, swapped, place, start=0, rows=PART):
    n = len(CHIPS)
    half = parts[0].shape[0] // 2
    pairs = [(parts[i].at[pl.ds(start, rows), :], place(i)) for i in range(n)]
    return pairs + [(swapped.at[pl.ds(i * half + start, rows), :], place(n + i)) for i in range(n)]


def collect_kernel(at_ref, *refs):
    n = len(CHIPS)
    ins, swapped, out, held, sems = refs[:n], refs[n], refs[n + 1], refs[n + 2], refs[n + 3]
    wide_at = at_ref[0]
    pairs = []
    for head in range(2):
        place = lambda i: held.at[head, source(wide_at, STEPS[i])]
        pairs += arrivals(ins, swapped, place, head * TAIL, TAIL)
    for copy in copy_all(pairs, sems):
        copy.wait()
    shape = (2 * SPAN_FAR, WIDE * TAIL)
    row, column = lax.broadcasted_iota(jnp.int32, shape, 0), lax.broadcasted_iota(jnp.int32, shape, 1)
    inner = row % SPAN_FAR
    wanted = (inner // FAR_ROWS) * TAIL + inner % FAR_ROWS + (row // SPAN_FAR) * FAR_ROWS
    choose = jnp.where(column == wanted, F32(1.0), F32(0.0)).astype(BF16)
    for head in range(2):
        rows = nn(choose, held[head].reshape(WIDE * TAIL, HEAD_DIM)).astype(BF16)
        lanes = slice(head * HEAD_DIM, (head + 1) * HEAD_DIM)
        out[:, :, lanes] = jnp.broadcast_to(rows[None], (NARROW, 2 * SPAN_FAR, HEAD_DIM))


def collect(at, parts, swapped):
    n = len(CHIPS)
    return pl.pallas_call(
        collect_kernel,
        out_shape=jax.ShapeDtypeStruct((NARROW, 2 * SPAN_FAR, PAIR), BF16),
        in_specs=[pl.BlockSpec(memory_space=pltpu.SMEM)] + [pl.BlockSpec(memory_space=pl.ANY)] * (n + 1),
        out_specs=pl.BlockSpec(memory_space=pltpu.VMEM),
        scratch_shapes=[pltpu.VMEM((2, WIDE, TAIL, HEAD_DIM), BF16), pltpu.SemaphoreType.DMA((2 * WIDE,))],
        compiler_params=pltpu.CompilerParams(vmem_limit_bytes=4 << 20),
        name="collect",
    )(at, *parts, swapped)


def highest(scores):
    return jnp.max(scores.reshape(scores.shape[0] // 8, 8, scores.shape[1]), axis=0)


def attend_kernel(at_ref, *refs):
    n = len(CHIPS)
    ins, swapped, far_ref, outs, far_out = refs[:n], refs[n], refs[n + 1], refs[n + 2 : 2 * n + 2], refs[2 * n + 2]
    held, kn_s, vn_s, o_s, dq_s, dk_s, dv_s, dkn_s, dvn_s, dkf_s, dvf_s, s_s, w_s, d_s, sems = refs[2 * n + 3 :]
    wide_at = at_ref[0]
    far_seen = at_ref[1] * SPAN_FAR
    copies = copy_all(arrivals(ins, swapped, lambda i: held.at[source(wide_at, STEPS[i])]), sems)
    for ref in (dk_s, dv_s, dkn_s, dvn_s, dkf_s, dvf_s):
        ref[...] = jnp.zeros(ref.shape, F32)
    for copy in copies:
        copy.wait()
    pool_near = pooling(NEAR_ROWS, NEAR)
    spread_near = spreading(NEAR_ROWS, NEAR)
    later = lax.broadcasted_iota(jnp.int32, (BLOCK, BLOCK), 0) > lax.broadcasted_iota(
        jnp.int32, (BLOCK, BLOCK), 1
    )
    far_blocked = lax.broadcasted_iota(jnp.int32, (FAR_ALL, 1), 0) >= far_seen
    far_bias = jnp.where(far_blocked, F32(BLOCKED), F32(0.0))
    exponent = SCALE * LOG2E
    wide2 = 2 * BLOCK
    for head in range(2):
        lanes = slice(head * HEAD_DIM, (head + 1) * HEAD_DIM)
        kf = far_ref[:, :SPAN_FAR, lanes].reshape(FAR_ALL, HEAD_DIM)
        vf = far_ref[:, SPAN_FAR:, lanes].reshape(FAR_ALL, HEAD_DIM)

        def rows_of(array, block):
            row = (2 * array + head) * BLOCK
            return held[block, row : row + BLOCK, :]

        key = functools.partial(rows_of, 0)
        value = functools.partial(rows_of, 1)
        query = functools.partial(rows_of, 2)
        grad = functools.partial(rows_of, 3)
        for block in range(WIDE):
            near_rows = slice(block * NEAR_ROWS, (block + 1) * NEAR_ROWS)
            kn_s[head, near_rows, :] = nn(pool_near, key(block)).astype(BF16)
            vn_s[head, near_rows, :] = nn(pool_near, value(block)).astype(BF16)
        for pair in range(WIDE // 2):
            blocks = (2 * pair, 2 * pair + 1)
            befores = tuple(max(b - 1, 0) for b in blocks)
            qs, gs = [query(b) for b in blocks], [grad(b) for b in blocks]
            q, g = jnp.concatenate(qs, axis=0), jnp.concatenate(gs, axis=0)
            near = 2 * NEAR_ROWS * pair + NEAR_ROWS
            far_from = wide2 + near
            total = far_from + FAR_ALL
            halves = [slice(b * BLOCK, (b + 1) * BLOCK) for b in range(2)]
            tops = []
            for b, cols in enumerate(halves):
                own = jnp.where(later, F32(BLOCKED), nt(key(blocks[b]), qs[b]))
                s_s[BLOCK:wide2, cols] = own
                tops.append(highest(own))
                if blocks[b] == 0:
                    s_s[0:BLOCK, cols] = jnp.full((BLOCK, BLOCK), BLOCKED, F32)
                else:
                    before = nt(key(befores[b]), qs[b])
                    s_s[0:BLOCK, cols] = before
                    tops[b] = jnp.maximum(tops[b], highest(before))
            top = jnp.concatenate(tops, axis=1)
            s_s[wide2:far_from, :] = nt(kn_s[head, 0:near, :], q)
            s_s[far_from - NEAR_ROWS : far_from, 0:BLOCK] = jnp.full((NEAR_ROWS, BLOCK), BLOCKED, F32)
            for i in range(0, FAR_ALL, BLOCK):
                scores = nt(kf[i : i + BLOCK, :], q) + far_bias[i : i + BLOCK]
                s_s[far_from + i : far_from + i + BLOCK, :] = scores
                top = jnp.maximum(top, highest(scores))
            chunks = [(0, BLOCK), (BLOCK, BLOCK)]
            chunks += [(wide2 + i, min(BLOCK, near - i)) for i in range(0, near, BLOCK)]
            chunks += [(far_from + i, BLOCK) for i in range(0, FAR_ALL, BLOCK)]
            top = jnp.maximum(top, highest(s_s[wide2:far_from, :]))
            top = jnp.max(top, axis=0, keepdims=True)
            norm = None
            for start, size in chunks:
                e = jnp.exp2((s_s[start : start + size, :] - top) * exponent)
                w_s[start : start + size, :] = e.astype(BF16)
                here = jnp.sum(e.reshape(size // 8, 8, wide2), axis=0)
                norm = here if norm is None else norm + here
            inverse = 1.0 / jnp.sum(norm, axis=0, keepdims=True)
            sides = [
                tn(value(befores[b]), w_s[0:BLOCK, cols]) + tn(value(blocks[b]), w_s[BLOCK:wide2, cols])
                for b, cols in enumerate(halves)
            ]
            attended = jnp.concatenate(sides, axis=1)
            attended += tn(vn_s[head, 0:near, :], w_s[wide2:far_from, :])
            attended += tn(vf, w_s[far_from:total, :])
            attended = (attended * inverse).astype(BF16).astype(F32)
            q_rows = slice(pair * wide2, (pair + 1) * wide2)
            o_s[head, q_rows, :] = attended.T.astype(BF16)
            grad_t = g.astype(F32).T
            row_dot = jnp.sum(grad_t * attended, axis=0, keepdims=True) * inverse
            g = (grad_t * inverse).T.astype(BF16)
            gs = [g[cols] for cols in halves]

            def put(start, size, cols, dprob, dot):
                d_s[start : start + size, cols] = (w_s[start : start + size, cols].astype(F32) * (dprob - dot)).astype(BF16)

            every = slice(0, wide2)
            for b, cols in enumerate(halves):
                put(0, BLOCK, cols, nt(value(befores[b]), gs[b]), row_dot[:, cols])
                put(BLOCK, BLOCK, cols, nt(value(blocks[b]), gs[b]), row_dot[:, cols])
            put(wide2, near, every, nt(vn_s[head, 0:near, :], g), row_dot)
            for i in range(0, FAR_ALL, BLOCK):
                put(far_from + i, BLOCK, every, nt(vf[i : i + BLOCK, :], g), row_dot)
            sides = []
            for b, cols in enumerate(halves):
                before, own = (slice(at * BLOCK, (at + 1) * BLOCK) for at in (befores[b], blocks[b]))
                sides.append(tn(key(befores[b]), d_s[0:BLOCK, cols]) + tn(key(blocks[b]), d_s[BLOCK:wide2, cols]))
                if blocks[b] > 0:
                    dk_s[head, before, :] += nn(d_s[0:BLOCK, cols], qs[b])
                    dv_s[head, before, :] += nn(w_s[0:BLOCK, cols], gs[b])
                dk_s[head, own, :] += nn(d_s[BLOCK:wide2, cols], qs[b])
                dv_s[head, own, :] += nn(w_s[BLOCK:wide2, cols], gs[b])
            grad_query = jnp.concatenate(sides, axis=1)
            grad_query += tn(kn_s[head, 0:near, :], d_s[wide2:far_from, :])
            grad_query += tn(kf, d_s[far_from:total, :])
            dq_s[head, q_rows, :] = (grad_query * SCALE).T.astype(BF16)
            dkn_s[head, 0:near, :] += nn(d_s[wide2:far_from, :], q)
            dvn_s[head, 0:near, :] += nn(w_s[wide2:far_from, :], g)
            dkf_s[head] += nn(d_s[far_from:total, :], q)
            dvf_s[head] += nn(w_s[far_from:total, :], g)

        far_out[:, :SPAN_FAR, lanes] = (dkf_s[head] * SCALE).astype(BF16).reshape(NARROW, SPAN_FAR, HEAD_DIM)
        far_out[:, SPAN_FAR:, lanes] = dvf_s[head].astype(BF16).reshape(NARROW, SPAN_FAR, HEAD_DIM)
        for block in range(WIDE):
            rows = slice(block * BLOCK, (block + 1) * BLOCK)
            near_rows = slice(block * NEAR_ROWS, (block + 1) * NEAR_ROWS)
            dk_s[head, rows, :] = (dk_s[head, rows, :] + nn(spread_near, dkn_s[head, near_rows, :].astype(BF16))) * SCALE
            dv_s[head, rows, :] = dv_s[head, rows, :] + nn(spread_near, dvn_s[head, near_rows, :].astype(BF16))
        for part, chip in enumerate(CHIPS):
            for core in range(2):
                rows = pl.ds(pl.multiple_of(target(wide_at, (chip, core)) * BLOCK, BLOCK), BLOCK)
                for i, ref in enumerate((o_s, dq_s, dk_s, dv_s)):
                    row = core * PART + (2 * i + head) * BLOCK
                    outs[part][row : row + BLOCK, :] = ref[head, rows, :].astype(BF16)


def attend(at, parts, swapped, far):
    n = len(CHIPS)
    vmem, some = pl.BlockSpec(memory_space=pltpu.VMEM), pl.BlockSpec(memory_space=pl.ANY)
    both = lambda rows, kind: pltpu.VMEM((2, rows, HEAD_DIM), kind)
    lists = lambda kind: pltpu.VMEM((SPAN, 2 * BLOCK), kind)
    outs = pl.pallas_call(
        attend_kernel,
        out_shape=[jax.ShapeDtypeStruct((2 * PART, HEAD_DIM), BF16)] * n
        + [jax.ShapeDtypeStruct((NARROW, 2 * SPAN_FAR, PAIR), BF16)],
        in_specs=[pl.BlockSpec(memory_space=pltpu.SMEM)] + [some] * (n + 1) + [vmem],
        out_specs=[vmem] * (n + 1),
        scratch_shapes=[pltpu.VMEM((WIDE, PART, HEAD_DIM), BF16)]
        + [both(SPAN_NEAR, BF16)] * 2 + [both(SPAN, BF16)] * 2 + [both(SPAN, F32)] * 2
        + [both(SPAN_NEAR, F32)] * 2 + [both(FAR_ALL, F32)] * 2
        + [lists(F32), lists(BF16), lists(BF16), pltpu.SemaphoreType.DMA((WIDE,))],
        compiler_params=pltpu.CompilerParams(vmem_limit_bytes=20 << 20),
        cost_estimate=pl.CostEstimate(flops=3_200_000_000, bytes_accessed=4 << 20, transcendentals=2 << 20),
        name="attend",
    )(at, *parts, swapped, far)
    return outs[:n], outs[n]


def total_kernel(at_ref, terms_ref, *outs):
    wide_at = at_ref[0]
    total = jnp.sum(terms_ref[...].astype(F32), axis=0).astype(BF16)
    shape = (TAIL, 2 * SPAN_FAR)
    row, column = lax.broadcasted_iota(jnp.int32, shape, 0), lax.broadcasted_iota(jnp.int32, shape, 1)
    for part, chip in enumerate(CHIPS):
        for core in range(2):
            first = target(wide_at, (chip, core)) * FAR_ROWS
            wanted = (row // FAR_ROWS) * SPAN_FAR + first + row % FAR_ROWS
            choose = jnp.where((column == wanted) & (row < 2 * FAR_ROWS), F32(1.0), F32(0.0)).astype(BF16)
            rows = nn(choose, total).astype(BF16)
            for head in range(2):
                at = (2 * core + head) * TAIL
                outs[part][at : at + TAIL, :] = rows[:, head * HEAD_DIM : (head + 1) * HEAD_DIM]


def total(at, terms):
    n = len(CHIPS)
    vmem = pl.BlockSpec(memory_space=pltpu.VMEM)
    return pl.pallas_call(
        total_kernel,
        out_shape=[jax.ShapeDtypeStruct((4 * TAIL, HEAD_DIM), BF16)] * n,
        in_specs=[pl.BlockSpec(memory_space=pltpu.SMEM), vmem],
        out_specs=[vmem] * n,
        compiler_params=pltpu.CompilerParams(vmem_limit_bytes=4 << 20),
        name="total",
    )(at, terms)


def unpack_kernel(at_ref, *refs):
    n = len(CHIPS)
    ins, swapped, tails, outs = refs[:n], refs[n], refs[n + 1 : 2 * n + 1], refs[2 * n + 1 : 2 * n + 5]
    held, far_s, sums, sems, far_sems, out_sems = refs[2 * n + 5 :]
    wide_at = at_ref[0]
    copies = copy_all(arrivals(ins, swapped, lambda i: held.at[i]), sems)
    rows = 2 * TAIL
    pairs = [(tails[i].at[pl.ds(0, rows), :], far_s.at[i]) for i in range(n)]
    pairs += [(swapped.at[pl.ds(n * PART + i * rows, rows), :], far_s.at[n + i]) for i in range(n)]
    for copy in copy_all(pairs, far_sems):
        copy.wait()
    for part, step in enumerate(STEPS):
        copies[part].wait()
        block = source(wide_at, step)
        for head in range(2):
            columns = pl.ds(pl.multiple_of(block * PAIR + head * HEAD_DIM, HEAD_DIM), HEAD_DIM)
            far = far_s[part, head * TAIL : (head + 1) * TAIL, :].astype(F32) * (1.0 / FAR)
            for i in range(4):
                row = (2 * i + head) * BLOCK
                piece = held[part, row : row + BLOCK, :]
                if i >= 2:
                    terms = piece.astype(F32)
                    at = (i - 2) * FAR_ROWS
                    both = [terms[r * FAR : (r + 1) * FAR] + far[at + r : at + r + 1] for r in range(FAR_ROWS)]
                    piece = jnp.concatenate(both, axis=0).astype(BF16)
                sums[i, :, columns] = piece
    strip = BLOCK // 4
    pairs = []
    for i in range(4):
        for r in range(0, BLOCK, strip):
            pairs.append((sums.at[i, r : r + strip, :], outs[i].at[r : r + strip, :]))
    for copy in copy_all(pairs, out_sems):
        copy.wait()


def unpack(at, parts, swapped, tails):
    n = len(CHIPS)
    some = pl.BlockSpec(memory_space=pl.ANY)
    return pl.pallas_call(
        unpack_kernel,
        out_shape=[jax.ShapeDtypeStruct((BLOCK, FEAT), BF16)] * 4,
        in_specs=[pl.BlockSpec(memory_space=pltpu.SMEM)] + [some] * (2 * n + 1),
        out_specs=[some] * 4,
        scratch_shapes=[
            pltpu.VMEM((WIDE, PART, HEAD_DIM), BF16),
            pltpu.VMEM((WIDE, 2 * TAIL, HEAD_DIM), BF16),
            pltpu.VMEM((4, BLOCK, FEAT), BF16),
            pltpu.SemaphoreType.DMA((WIDE,)),
            pltpu.SemaphoreType.DMA((WIDE,)),
            pltpu.SemaphoreType.DMA((16,)),
        ],
        compiler_params=pltpu.CompilerParams(vmem_limit_bytes=8 << 20),
        name="unpack",
    )(at, *parts, swapped, *tails)


def shards(queries, keys, values, grad_out):
    at = jnp.stack([lax.axis_index("wide"), lax.axis_index("narrow")]).astype(jnp.int32)
    tails = to_chips(tails_of(at, keys, values))
    parts = pack(at, queries, keys, values, grad_out)
    tails, parts = lax.optimization_barrier((list(tails), list(parts)))
    swapped = to_other_core(tails)
    swapped, *parts = lax.optimization_barrier((swapped, *parts))
    parts = to_chips_in_turn(parts)
    far = lax.all_to_all(collect(at, tails, swapped), "narrow", 0, 0, tiled=True)
    far, *parts = lax.optimization_barrier((far, *parts))
    outs, terms = attend(at, parts, to_other_core(parts), far)
    outs = to_chips_in_turn(outs)
    tails = to_chips(total(at, lax.all_to_all(terms, "narrow", 0, 0, tiled=True)))
    return tuple(unpack(at, outs, to_other_core([*outs, *tails]), tails))


def solution(mesh):
    rows = P(("narrow", "wide"), None)
    return jax.shard_map(
        shards, mesh=mesh, in_specs=(rows,) * 4, out_specs=(rows,) * 4, check_vma=False
    )
```
